256 devices in a mesh: dp: 8 (over x, core), expert: 32 (over y, z).
Axes of the slice: x: 4, y: 4, z: 8, core: 2. Of those that a mesh axis runs over, the one named last changes fastest.
Arguments:
- queries: bfloat16 [256, 128, 4096], P(('dp', 'expert')), may hold values from -120 to 120
- key_rows: bfloat16 [256, 128, 256], P(('dp', 'expert')), may hold values from -6 to 6
- value_matrix: bfloat16 [256, 128, 256], P(('dp', 'expert')), may hold values from -6 to 6
- doc_lengths: int32 [32, 8, 4], P('expert'), may hold values from 1 to 64, 128 in all within a row
- seq_plan: int32 [32, 8], P('expert'), may hold values from 0 to 7, as said below
- norm_gain: float32 [4096], replicated, may hold values from 0.5 to 1.5
- w_gate: bfloat16 [32, 4096, 192], P('expert'), may hold values from -0.09375 to 0.09375
- w_up: bfloat16 [32, 4096, 192], P('expert'), may hold values from -0.09375 to 0.09375
- w_down: bfloat16 [32, 192, 4096], P('expert'), may hold values from -0.15625 to 0.15625
- expert_ids: int32 [256, 128, 8], P(('dp', 'expert')), may hold values from 0 to 127, all different within a row; in each aligned block of 128 rows (0 to 127, 128 to 255, ..., all dimensions but the last counted through in order) at most 14 rows name the same one
- gate_weights: float32 [256, 128, 8], P(('dp', 'expert')), may hold values from 0.1 to 1
- out_grad: bfloat16 [256, 128, 4096], P(('dp', 'expert')), may hold values from -6 to 6
Outputs:
- layer_out: bfloat16 [256, 128, 4096], P(('dp', 'expert'))
- grad_queries: bfloat16 [256, 128, 4096], P(('dp', 'expert'))
- grad_keys: bfloat16 [256, 128, 256], P(('dp', 'expert'))
- grad_values: bfloat16 [256, 128, 256], P(('dp', 'expert'))
The draws below stay inside these ranges and needn't reach their ends.
Inputs may be any that keep to these rules, and one draw needn't show every extreme that they name: `expert_ids`: in each device's block of 128 token slots no expert id is named by more than 14 slots, a bound that some block reaches. `seq_plan`: each row maps dp rank d to d XOR m, with one mask m of that row between 1 and 8 - 1. `doc_lengths`: each row of 4 lengths sums to 128.
All inputs are finite; a program needn't handle non-finite values.
Results may differ from the reference program's by a relative error of at most 0.019.
Values may be sent and summed in bfloat16 or wider, within the bound.
No kernel may reach another device: no remote copies, remote signals or barrier semaphores. Data moves between devices by JAX's collectives and lax.ppermute only.
A program may use at most 128 MiB of HBM per device.

```python
import math
import jax
import jax.numpy as jnp
import numpy as np
from jax import lax

D = 4096
HEAD_SIZE = 128
QUERY_HEADS = 32
KEY_VALUE_HEADS = 2
FF = 1536
ALL_EXP = 128
TOPK = 8
GROUP = 8
DOCS = 4
TOKENS_PER_SEQ = 128
SLICE = 192
EXPERTS = 4
CAP = 14
SEQUENCE_TOTAL = 256
N_DP = 8
N_EXPERT = 32


def shared_keys(key):
    return jnp.clip(jax.random.normal(key, (SEQUENCE_TOTAL, TOKENS_PER_SEQ, KEY_VALUE_HEADS * HEAD_SIZE), jnp.float32), -5.0, 5.0)


def draw_key_rows(key, part):
    base_offset = shared_keys(key)
    return base_offset.astype(jnp.bfloat16)


def draw_queries(key, part):
    key = jax.random.fold_in(key, 7)
    own = jnp.clip(jax.random.normal(key, (SEQUENCE_TOTAL, TOKENS_PER_SEQ, QUERY_HEADS * HEAD_SIZE), jnp.float32), -6.0, 6.0)
    return own.astype(jnp.bfloat16)


def draw_seq_plan(key, part):
    key = jax.random.fold_in(key, 5)
    masks = jax.random.randint(key, (N_EXPERT, 1), 1, N_DP, dtype=jnp.int32)
    ranks = jnp.arange(N_DP, dtype=jnp.int32)[None, :]
    return jnp.bitwise_xor(ranks, masks).astype(jnp.int32)


def steps_of(rng, dims, shards, least, top_value):
    def one(dim, parts):
        draws = jax.random.uniform(jax.random.fold_in(jax.random.fold_in(rng, 6), dim), (parts,), jnp.float32, least / len(shards), top_value / len(shards))
        return jnp.repeat(jnp.exp(draws), dims[dim] // parts).reshape((-1,) + (1,) * (len(dims) - dim - 1))

    factor_of = one(*shards[0])
    for cut in shards[1:]:
        factor_of = factor_of * one(*cut)
    return factor_of


def split_up(count, total, reach, lean):
    weights = [(1 << 20) // math.isqrt(rank ** lean) + 1 for rank in range(2, count + 1)]
    surplus, counts = total - reach - (count - 1), [1] * (count - 1)
    while surplus > 0:
        movable = [i for i in range(count - 1) if counts[i] < reach]
        whole, left = sum([weights[i] for i in movable]), surplus
        for i in movable:
            addition = min(reach - counts[i], max(1, left * weights[i] // whole), surplus)
            counts[i] = counts[i] + addition
            surplus = surplus - addition
    return np.array([reach] + counts)


def ragged_sizes(rng, number_of, total, most, lean):
    if number_of == 2:
        one = jax.random.randint(rng, (), max(1, total - most), min(most, total - 1) + 1)
        return jnp.stack([one, total - one])
    sizes = jnp.asarray(split_up(number_of, total, most, lean), jnp.int32)
    twos = (number_of - 1) // 2
    source_of, sink = sizes[1:1 + 2 * twos:2], sizes[2:2 + 2 * twos:2]
    margin = jnp.minimum(source_of - 1, most - sink)
    moved = jax.random.randint(jax.random.fold_in(rng, 1), (twos,), 0, 1 << 20) % (margin + 1)
    sizes = sizes.at[1:1 + 2 * twos:2].set(source_of - moved).at[2:2 + 2 * twos:2].set(sink + moved)
    return sizes[jax.random.permutation(jax.random.fold_in(rng, 2), number_of)]


def assign_block(own_key, own, number, rows, number_of, top, most, skew):
    order = jax.random.permutation(own_key, number_of)
    packed, ordinary = load_shares(number_of, rows * top, most, skew, True), load_shares(number_of, rows * top, most, skew, False)
    places = jnp.arange(number_of)

    def named(lengths, turn):
        used = int((lengths > 0).sum())
        fixed = max(1, used // 4)
        passed = fixed + (places - fixed + turn * (used - fixed)) % max(1, number_of - fixed)
        return jnp.zeros((number_of,), jnp.int32).at[order[jnp.where(places < fixed, places, passed)]].set(jnp.asarray(lengths, jnp.int32))

    lengths = jnp.where(number % 4 == 0, named(packed, number // 4), named(ordinary, number - number // 4 - 1))
    mixed = jax.random.permutation(jax.random.fold_in(own, 3), number_of)
    donor, receiver = mixed[0:number_of // 2 * 2:2], mixed[1:number_of // 2 * 2:2]
    slack = jnp.minimum(lengths[donor] - 1, most - lengths[receiver]) // 2
    slack = jnp.where((donor == order[0]) | (receiver == order[0]) | (lengths[receiver] == 0), 0, jnp.maximum(slack, 0))
    passed = jax.random.randint(jax.random.fold_in(own, 4), (number_of // 2,), 0, 1 << 20) % (slack + 1)
    lengths = lengths.at[donor].add(-passed).at[receiver].add(passed)
    labels = jnp.searchsorted(jnp.cumsum(lengths), jnp.arange(rows * top), side="right").astype(jnp.int32)
    grid = labels.reshape(top, rows).T
    grid = grid[jax.random.permutation(jax.random.fold_in(own, 1), rows)]
    turn = jax.random.randint(jax.random.fold_in(own, 2), (rows, 1), 0, top)
    return jnp.take_along_axis(grid, (jnp.arange(top)[None, :] + turn) % top, axis=1)


def load_shares(amount, total, reach, skew, full):
    portions = [(1 << 20) // math.isqrt(grade ** skew) + 1 for grade in range(1, amount + 1)]
    largest = reach if full else min(reach, max(-(-total // amount), total * portions[0] // sum(portions)))
    least = 1 if total - largest >= amount - 1 else 0
    counts, rest = [largest] + [least] * (amount - 1), total - largest - least * (amount - 1)
    while rest > 0:
        candidates = [i for i in range(1, amount) if counts[i] < largest] or [i for i in range(1, amount) if counts[i] < reach]
        pool, budget = sum([portions[i] for i in candidates]), rest
        for i in candidates:
            extra = min(reach - counts[i], max(1, budget * portions[i] // pool), rest)
            counts[i] = counts[i] + extra
            rest = rest - extra
    return np.array(counts)


def bell_draw(stream_key, shape, deviation, reach, shards=(), kind=jnp.bfloat16):
    level = steps_of(stream_key, shape, shards, -0.22, 0.18) if shards else 1.0
    drawn = jax.random.normal(stream_key, shape, jnp.float32) * deviation * level
    return jnp.minimum(jnp.maximum(drawn, -reach), reach).astype(kind)


def setup_inputs(seed: int = 0) -> dict:
    splits = jax.random.split(jax.random.key(seed), 13)
    queries = draw_queries(jax.random.fold_in(splits[12], 71), 0)
    key_rows = draw_key_rows(jax.random.fold_in(splits[12], 71), 0)
    value_matrix = bell_draw(splits[2], (SEQUENCE_TOTAL, TOKENS_PER_SEQ, KEY_VALUE_HEADS * HEAD_SIZE), 1.0, 6.0, ((0, 256),))
    doc_lengths = jax.vmap(lambda own: ragged_sizes(own, DOCS, TOKENS_PER_SEQ, TOKENS_PER_SEQ // 2, 2))(jax.random.split(splits[3], N_EXPERT * N_DP)).reshape((N_EXPERT, N_DP, DOCS)).astype(jnp.int32)
    seq_plan = draw_seq_plan(jax.random.fold_in(splits[12], 71), 0)
    norm_gain = jnp.clip(jax.random.uniform(splits[5], (D,), jnp.float32, 0.5, 1.5), 0.5, 1.5)
    w_gate = bell_draw(splits[6], (N_EXPERT, D, SLICE), D ** -0.5, 0.09375, ((0, 32),))
    w_up = bell_draw(splits[7], (N_EXPERT, D, SLICE), D ** -0.5, 0.09375, ((0, 32),))
    w_down = bell_draw(splits[8], (N_EXPERT, SLICE, D), FF ** -0.5, 0.15625, ((0, 32),))
    expert_ids_keys = jax.random.split(jax.random.fold_in(splits[9], 1), SEQUENCE_TOTAL * TOKENS_PER_SEQ // TOKENS_PER_SEQ)
    expert_ids_turns = jax.random.permutation(jax.random.fold_in(splits[9], 3), SEQUENCE_TOTAL * TOKENS_PER_SEQ // TOKENS_PER_SEQ)
    expert_ids = jax.vmap(lambda own, number: assign_block(jax.random.fold_in(splits[9], 2), own, number, TOKENS_PER_SEQ, ALL_EXP, TOPK, CAP, 2))(expert_ids_keys, expert_ids_turns).reshape((SEQUENCE_TOTAL, TOKENS_PER_SEQ, TOPK))
    gate_weights = jnp.clip(jnp.exp(math.log(1.0) - 2.3025851 * jax.random.uniform(splits[10], (SEQUENCE_TOTAL, TOKENS_PER_SEQ, TOPK), jnp.float32) ** steps_of(splits[10], (SEQUENCE_TOTAL, TOKENS_PER_SEQ, TOPK), ((0, 256),), -0.2, 0.2)), 0.1, 1.0)
    out_grad = bell_draw(splits[11], (SEQUENCE_TOTAL, TOKENS_PER_SEQ, D), 1.0, 6.0, ((0, 256),))
    return dict(queries=queries, key_rows=key_rows, value_matrix=value_matrix, doc_lengths=doc_lengths, seq_plan=seq_plan, norm_gain=norm_gain, w_gate=w_gate, w_up=w_up, w_down=w_down, expert_ids=expert_ids, gate_weights=gate_weights, out_grad=out_grad)


def doc_index(lengths_row, count):
    bounds = jnp.cumsum(lengths_row)
    places = jnp.arange(count, dtype=jnp.int32)
    return lax.optimization_barrier(jnp.sum((places[:, None] >= bounds[None, :]).astype(jnp.int32), axis=1))

def attend(queries, key_rows, value_matrix, docs):
    count = queries.shape[0]
    head_group = QUERY_HEADS // KEY_VALUE_HEADS
    scale = HEAD_SIZE ** (-0.5)
    places = jnp.arange(count, dtype=jnp.int32)
    allowed = (docs[:, None] == docs[None, :]) & (places[None, :] <= places[:, None])
    outputs = []
    weights = []
    for head_slot in range(KEY_VALUE_HEADS):
        q_part = queries[:, head_slot * head_group * HEAD_SIZE:(head_slot + 1) * head_group * HEAD_SIZE].reshape(count, head_group, HEAD_SIZE).astype(jnp.float32)
        k_part = key_rows[:, head_slot * HEAD_SIZE:(head_slot + 1) * HEAD_SIZE].astype(jnp.float32)
        v_part = value_matrix[:, head_slot * HEAD_SIZE:(head_slot + 1) * HEAD_SIZE].astype(jnp.float32)
        scores = jnp.einsum('tgd,sd->gts', q_part, k_part) * scale
        scores = jnp.where(allowed[None], scores, -1e+30)
        peak = lax.optimization_barrier(jnp.max(scores, axis=-1, keepdims=True))
        expo = jnp.exp(scores - peak)
        probs = (expo / lax.optimization_barrier(jnp.sum(expo, axis=-1, keepdims=True))).astype(jnp.bfloat16)
        probs = lax.optimization_barrier(probs)
        mixed = jnp.einsum('gts,sd->tgd', probs.astype(jnp.float32), v_part)
        outputs.append(mixed.reshape(count, head_group * HEAD_SIZE))
        weights.append(probs)
    return (jnp.concatenate(outputs, axis=1).astype(jnp.bfloat16), weights)

def attend_back(queries, key_rows, value_matrix, docs, attn_grad):
    attn, weights = attend(queries, key_rows, value_matrix, docs)
    count = queries.shape[0]
    head_group = QUERY_HEADS // KEY_VALUE_HEADS
    scale = HEAD_SIZE ** (-0.5)
    q_grads = []
    k_grads = []
    v_grads = []
    for head_slot in range(KEY_VALUE_HEADS):
        span = slice(head_slot * head_group * HEAD_SIZE, (head_slot + 1) * head_group * HEAD_SIZE)
        q_part = queries[:, span].reshape(count, head_group, HEAD_SIZE).astype(jnp.float32)
        k_part = key_rows[:, head_slot * HEAD_SIZE:(head_slot + 1) * HEAD_SIZE].astype(jnp.float32)
        v_part = value_matrix[:, head_slot * HEAD_SIZE:(head_slot + 1) * HEAD_SIZE].astype(jnp.float32)
        d_part = attn_grad[:, span].reshape(count, head_group, HEAD_SIZE).astype(jnp.float32)
        o_part = attn[:, span].reshape(count, head_group, HEAD_SIZE).astype(jnp.float32)
        probs = weights[head_slot].astype(jnp.float32)
        v_grads.append(jnp.einsum('gts,tgd->sd', probs, d_part))
        prob_grad = jnp.einsum('tgd,sd->gts', d_part, v_part)
        inner = jnp.transpose(lax.optimization_barrier(jnp.sum(d_part * o_part, axis=-1)))[:, :, None]
        score_grad = (probs * (prob_grad - inner) * scale).astype(jnp.bfloat16)
        score_grad = lax.optimization_barrier(score_grad).astype(jnp.float32)
        q_grads.append(jnp.einsum('gts,sd->tgd', score_grad, k_part).reshape(count, head_group * HEAD_SIZE))
        k_grads.append(jnp.einsum('gts,tgd->sd', score_grad, q_part))
    return (jnp.concatenate(q_grads, axis=1).astype(jnp.bfloat16), jnp.concatenate(k_grads, axis=1).astype(jnp.bfloat16), jnp.concatenate(v_grads, axis=1).astype(jnp.bfloat16))

def reference(queries, key_rows, value_matrix, doc_lengths, seq_plan, norm_gain, w_gate, w_up, w_down, expert_ids, gate_weights, out_grad):
    count = TOKENS_PER_SEQ
    seq_lengths = jnp.transpose(doc_lengths, (1, 0, 2)).reshape(SEQUENCE_TOTAL, DOCS)
    docs = jax.vmap(lambda row: doc_index(row, count))(seq_lengths)
    attn = lax.map(lambda item: attend(item[0], item[1], item[2], item[3])[0], (queries, key_rows, value_matrix, docs))
    rank_ids = jnp.arange(N_DP, dtype=jnp.int32)
    columns = jnp.arange(N_EXPERT, dtype=jnp.int32)
    matches = seq_plan[:, :, None] == rank_ids[None, None, :]
    anchor = lax.optimization_barrier(jnp.sum(jnp.where(matches, rank_ids[None, :, None], 0), axis=1)).astype(jnp.int32)
    home_four = attn.reshape(N_DP, N_EXPERT, count, QUERY_HEADS * HEAD_SIZE)
    moved = home_four[jnp.transpose(anchor), columns[None, :]].reshape(SEQUENCE_TOTAL * count, D)
    moved32 = moved.astype(jnp.float32)
    gain = norm_gain.astype(jnp.float32)
    scaling = lax.rsqrt(lax.optimization_barrier(jnp.mean(moved32 * moved32, axis=-1, keepdims=True)) + 1e-06)
    normed = (moved32 * scaling * gain).astype(jnp.bfloat16)
    route_ids = expert_ids.reshape(-1, TOPK)
    route_gates = gate_weights.reshape(-1, TOPK).astype(jnp.float32)
    grad_rows = out_grad.reshape(-1, D)
    total_add = jnp.zeros((SEQUENCE_TOTAL * count, D), jnp.float32)
    total_grad = jnp.zeros((SEQUENCE_TOTAL * count, D), jnp.float32)
    limit = SEQUENCE_TOTAL * CAP
    for expert in range(EXPERTS):
        hits = route_ids == expert
        present = jnp.any(hits, axis=-1)
        weight = lax.optimization_barrier(jnp.sum(jnp.where(hits, route_gates, 0.0), axis=-1))
        number = jnp.sum(present.astype(jnp.int32))
        picks = jnp.nonzero(present, size=limit, fill_value=0)[0].astype(jnp.int32)
        live = (jnp.arange(limit, dtype=jnp.int32) < number).astype(jnp.float32)
        row_weight = weight[picks] * live
        rows = normed[picks]
        pair_grad = (row_weight[:, None] * grad_rows[picks].astype(jnp.float32)).astype(jnp.bfloat16)
        block = slice(expert * GROUP, (expert + 1) * GROUP)
        gate_full = jnp.transpose(w_gate[block], (1, 0, 2)).reshape(D, FF)
        up_full = jnp.transpose(w_up[block], (1, 0, 2)).reshape(D, FF)
        down_full = w_down[block].reshape(FF, D)
        gate_in = jnp.dot(rows, gate_full, preferred_element_type=jnp.float32)
        up_in = jnp.dot(rows, up_full, preferred_element_type=jnp.float32)
        sigma = jax.nn.sigmoid(gate_in)
        active = gate_in * sigma
        hidden = (active * up_in).astype(jnp.bfloat16)
        hidden_grad = jnp.dot(pair_grad, jnp.transpose(down_full), preferred_element_type=jnp.float32)
        gate_grad = (hidden_grad * up_in * sigma * (1.0 + gate_in * (1.0 - sigma))).astype(jnp.bfloat16)
        up_grad = (hidden_grad * active).astype(jnp.bfloat16)
        expert_out = jnp.zeros((limit, D), jnp.float32)
        normed_grad = jnp.zeros((limit, D), jnp.float32)
        for piece in range(GROUP):
            span = slice(piece * SLICE, (piece + 1) * SLICE)
            index = expert * GROUP + piece
            share = jnp.dot(hidden[:, span], w_down[index], preferred_element_type=jnp.float32).astype(jnp.bfloat16)
            expert_out = expert_out + lax.optimization_barrier(share).astype(jnp.float32)
            back = jnp.dot(gate_grad[:, span], jnp.transpose(w_gate[index]), preferred_element_type=jnp.float32)
            back = back + jnp.dot(up_grad[:, span], jnp.transpose(w_up[index]), preferred_element_type=jnp.float32)
            back = back.astype(jnp.bfloat16)
            normed_grad = normed_grad + lax.optimization_barrier(back).astype(jnp.float32)
        total_add = total_add.at[picks].add(row_weight[:, None] * expert_out)
        total_grad = total_grad.at[picks].add(live[:, None] * normed_grad)
    layer_out = (moved32 + total_add).astype(jnp.bfloat16)
    mean_term = lax.optimization_barrier(jnp.mean(moved32 * gain * total_grad, axis=-1, keepdims=True))
    moved_grad = grad_rows.astype(jnp.float32) + scaling * gain * total_grad - moved32 * scaling ** 3 * mean_term
    moved_grad = moved_grad.astype(jnp.bfloat16)
    grad_four = moved_grad.reshape(N_DP, N_EXPERT, count, QUERY_HEADS * HEAD_SIZE)
    attn_grad = grad_four[jnp.transpose(seq_plan), columns[None, :]].reshape(SEQUENCE_TOTAL, count, QUERY_HEADS * HEAD_SIZE)
    grad_queries, grad_keys, grad_values = lax.map(lambda item: attend_back(item[0], item[1], item[2], item[3], item[4]), (queries, key_rows, value_matrix, docs, attn_grad))
    return (layer_out.reshape(SEQUENCE_TOTAL, count, D), grad_queries, grad_keys, grad_values)
```

```python
import jax
import jax.numpy as jnp
from jax import lax
from jax.sharding import Mesh
from jax.sharding import PartitionSpec as P

HEAD_SIZE = 128
QUERY_HEADS = 32
KEY_VALUE_HEADS = 2
GROUP = 8
CAP = 14
EXPERTS = 4
F32 = jnp.float32
BF16 = jnp.bfloat16


def doc_index(lengths_row, count):
    bounds = jnp.cumsum(lengths_row)
    places = jnp.arange(count, dtype=jnp.int32)
    return jnp.sum((places[:, None] >= bounds[None, :]).astype(jnp.int32), axis=1)


def attend(queries, key_rows, value_matrix, docs):
    count = queries.shape[0]
    head_group = QUERY_HEADS // KEY_VALUE_HEADS
    scale = HEAD_SIZE ** (-0.5)
    places = jnp.arange(count, dtype=jnp.int32)
    allowed = (docs[:, None] == docs[None, :]) & (places[None, :] <= places[:, None])
    outputs = []
    weights = []
    for head_slot in range(KEY_VALUE_HEADS):
        q_part = queries[
            :, head_slot * head_group * HEAD_SIZE : (head_slot + 1) * head_group * HEAD_SIZE
        ].reshape(count, head_group, HEAD_SIZE)
        k_part = key_rows[:, head_slot * HEAD_SIZE : (head_slot + 1) * HEAD_SIZE]
        v_part = value_matrix[:, head_slot * HEAD_SIZE : (head_slot + 1) * HEAD_SIZE]
        scores = jnp.einsum("tgd,sd->gts", q_part, k_part, preferred_element_type=F32) * scale
        scores = jnp.where(allowed[None], scores, -1e30)
        peak = jnp.max(scores, axis=-1, keepdims=True)
        expo = jnp.exp(scores - peak)
        probs = (expo / jnp.sum(expo, axis=-1, keepdims=True)).astype(BF16)
        mixed = jnp.einsum("gts,sd->tgd", probs, v_part, preferred_element_type=F32)
        outputs.append(mixed.reshape(count, head_group * HEAD_SIZE))
        weights.append(probs)
    return (jnp.concatenate(outputs, axis=1).astype(BF16), weights)


def attend_back(queries, key_rows, value_matrix, weights, attn, attn_grad):
    count = queries.shape[0]
    head_group = QUERY_HEADS // KEY_VALUE_HEADS
    scale = HEAD_SIZE ** (-0.5)
    q_grads = []
    k_grads = []
    v_grads = []
    for head_slot in range(KEY_VALUE_HEADS):
        span = slice(head_slot * head_group * HEAD_SIZE, (head_slot + 1) * head_group * HEAD_SIZE)
        q_part = queries[:, span].reshape(count, head_group, HEAD_SIZE)
        k_part = key_rows[:, head_slot * HEAD_SIZE : (head_slot + 1) * HEAD_SIZE]
        v_part = value_matrix[:, head_slot * HEAD_SIZE : (head_slot + 1) * HEAD_SIZE]
        d_part = attn_grad[:, span].reshape(count, head_group, HEAD_SIZE)
        o_part = attn[:, span].reshape(count, head_group, HEAD_SIZE)
        probs = weights[head_slot]
        v_grads.append(jnp.einsum("gts,tgd->sd", probs, d_part, preferred_element_type=F32))
        prob_grad = jnp.einsum("tgd,sd->gts", d_part, v_part, preferred_element_type=F32)
        inner = jnp.sum(d_part.astype(F32) * o_part.astype(F32), axis=-1)
        inner = jnp.transpose(inner)[:, :, None]
        score_grad = (probs.astype(F32) * (prob_grad - inner) * scale).astype(BF16)
        q_grads.append(
            jnp.einsum("gts,sd->tgd", score_grad, k_part, preferred_element_type=F32).reshape(
                count, head_group * HEAD_SIZE
            )
        )
        k_grads.append(jnp.einsum("gts,tgd->sd", score_grad, q_part, preferred_element_type=F32))
    return (
        jnp.concatenate(q_grads, axis=1).astype(BF16),
        jnp.concatenate(k_grads, axis=1).astype(BF16),
        jnp.concatenate(v_grads, axis=1).astype(BF16),
    )


def shifted(value, axis, step):
    size = lax.axis_size(axis)
    if step % size == 0:
        return value
    return lax.ppermute(value, axis, [(i, (i + step) % size) for i in range(size)])


def swapped(value):
    return lax.ppermute(value, "c", [(0, 1), (1, 0)])


def to_experts(blocks):
    return [shifted(blocks[s], "y", s) for s in range(EXPERTS)]


def from_experts(blocks):
    return [shifted(blocks[s], "y", -s) for s in range(EXPERTS)]


def gather_rows(block):
    size = lax.axis_size("x")
    mine = [shifted(block, "x", s) for s in range(size)]
    other = [swapped(b) for b in mine]
    return jnp.concatenate(mine + other, axis=0)


def scatter_sums(parts):
    size = lax.axis_size("x")
    half = parts.shape[0] // 2
    each = half // size
    both = (parts[:half].astype(F32) + swapped(parts[half:]).astype(F32)).astype(BF16)
    total = both[:each].astype(F32)
    for s in range(1, size):
        total = total + shifted(both[s * each : (s + 1) * each], "x", -s).astype(F32)
    return total.astype(BF16)


def nt(left, right):
    return lax.dot_general(left, right, (((1,), (1,)), ((), ())), preferred_element_type=F32)


def tn(left, right):
    return lax.dot_general(left, right, (((0,), (0,)), ((), ())), preferred_element_type=F32)


def nn(left, right):
    return jnp.dot(left, right, preferred_element_type=F32)


def by_mask(mask, move):
    ranks = lax.axis_size("x") * lax.axis_size("c")

    def branch(k):
        pairs = [(i, i ^ k) for i in range(ranks)]
        return lambda: move(lambda v: lax.ppermute(v, ("x", "c"), pairs))

    return lax.switch(mask - 1, [branch(k) for k in range(1, ranks)])


def shards(
    queries,
    key_rows,
    value_matrix,
    doc_lengths,
    seq_plan,
    norm_gain,
    w_gate,
    w_up,
    w_down,
    expert_ids,
    gate_weights,
    out_grad,
):
    queries, key_rows, value_matrix, out_grad = queries[0], key_rows[0], value_matrix[0], out_grad[0]
    w_gate, w_up, w_down = w_gate[0], w_up[0], w_down[0]
    route_ids, route_gates = expert_ids[0], gate_weights[0]
    x, c, y = lax.axis_index("x"), lax.axis_index("c"), lax.axis_index("y")
    x_size = lax.axis_size("x")
    ranks = 2 * x_size
    rank = x * 2 + c
    count, width = queries.shape
    mask = seq_plan[0, 0]

    units = w_gate.shape[1] // ranks
    pick = (
        jnp.arange(w_gate.shape[1], dtype=jnp.int32)[None, :]
        == rank * units + jnp.arange(units, dtype=jnp.int32)[:, None]
    ).astype(BF16)
    gate_piece = nt(pick, w_gate).astype(BF16)
    up_piece = nt(pick, w_up).astype(BF16)
    down_piece = lax.dynamic_slice_in_dim(w_down, rank * units, units, 0)
    pieces = jnp.stack([gate_piece, up_piece, down_piece])
    mats = lax.all_gather(pieces, "z", axis=1, tiled=True)

    experts = (y + jnp.arange(EXPERTS, dtype=jnp.int32)) % EXPERTS
    hits = (route_ids[:, :, None] == experts[None, None, :]).astype(F32)
    present = jnp.sum(hits, axis=1)
    weight = jnp.sum(route_gates[:, :, None] * hits, axis=1)
    places = jnp.arange(count, dtype=jnp.int32)
    earlier = (places[None, :] < places[:, None]).astype(BF16)
    counts = nn(earlier, present.astype(BF16))
    code = jnp.transpose(jnp.where(present > 0.5, counts, -1.0))
    slot_ids = jnp.arange(CAP, dtype=F32)
    select = code[:, None, :] == slot_ids[None, :, None]
    select_half = select.astype(BF16).reshape(EXPERTS * CAP, count)
    spread = jnp.where(select, jnp.transpose(weight)[:, None, :], 0.0).reshape(EXPERTS * CAP, count)
    slot_weight = jnp.sum(spread, axis=1, keepdims=True)
    pair_grad = (slot_weight * nn(select_half, out_grad)).astype(BF16)
    pair_blocks = to_experts(pair_grad.reshape(EXPERTS, CAP, width))
    masks = jnp.stack([v[0, 0] for v in to_experts([jnp.full((8, 128), mask)] * EXPERTS)])

    lengths = lax.dynamic_index_in_dim(doc_lengths[0], rank, 0, keepdims=False)
    home_docs = doc_index(lengths, count)

    def forward(move):
        grad_home, code_home = move(out_grad), move(code)
        attn, weights = attend(queries, key_rows, value_matrix, home_docs)
        return grad_home, code_home, attn, weights

    grad_home, code_home, attn, weights = by_mask(mask, forward)

    moved32 = attn.astype(F32)
    scaling = lax.rsqrt(jnp.mean(moved32 * moved32, axis=-1, keepdims=True) + 1e-06)
    normed = (moved32 * scaling * norm_gain).astype(BF16)
    select_home = (
        (code_home[:, None, :] == slot_ids[None, :, None])
        .astype(BF16)
        .reshape(EXPERTS * CAP, count)
    )
    rows = nn(select_home, normed).astype(BF16)
    row_blocks = to_experts(rows.reshape(EXPERTS, CAP, width))

    grads = gather_rows(jnp.concatenate(pair_blocks, axis=0))
    rows = gather_rows(jnp.concatenate(row_blocks, axis=0))

    index = jnp.arange(2 * x_size * EXPERTS * CAP, dtype=jnp.int32)
    turn = (index // CAP) % EXPERTS
    far = (index // (CAP * EXPERTS)) % x_size
    flip = index // (CAP * EXPERTS * x_size)
    owner = ((x - far) % x_size) * 2 + (c ^ flip)
    tail = turn * CAP + index % CAP
    slot_key = owner * (EXPERTS * CAP) + tail
    masks_of = jnp.sum(
        jnp.where(turn[:, None] == jnp.arange(EXPERTS)[None, :], masks[None, :], 0), axis=1
    )
    home_key = (owner ^ masks_of) * (EXPERTS * CAP) + tail
    match = home_key[:, None] == slot_key[None, :]

    gate_in = nt(rows, mats[0])
    up_in = nt(rows, mats[1])
    hidden_grad = jnp.dot(match.astype(F32), nt(grads, mats[2]), precision=lax.Precision.HIGHEST)
    sigma = jax.nn.sigmoid(gate_in)
    active = gate_in * sigma
    hidden = (active * up_in).astype(BF16)
    hidden = tn(match.astype(BF16), hidden).astype(BF16)
    part_out = nn(hidden, mats[2]).astype(BF16)
    gate_grad = (hidden_grad * up_in * sigma * (1.0 + gate_in * (1.0 - sigma))).astype(BF16)
    up_grad = (hidden_grad * active).astype(BF16)
    part_in = (nn(gate_grad, mats[0]) + nn(up_grad, mats[1])).astype(BF16)

    in_sum = scatter_sums(part_in).reshape(EXPERTS, CAP, width)
    in_rows = jnp.concatenate(from_experts(in_sum), axis=0)
    out_sum = scatter_sums(part_out).reshape(EXPERTS, CAP, width)
    out_rows = jnp.concatenate(from_experts(out_sum), axis=0)

    def backward(move):
        moved = move(attn)
        normed_grad = tn(select_home, in_rows)
        mean_term = jnp.mean(moved32 * norm_gain * normed_grad, axis=-1, keepdims=True)
        attn_grad = (
            grad_home.astype(F32)
            + scaling * norm_gain * normed_grad
            - moved32 * scaling**3 * mean_term
        ).astype(BF16)
        return (moved, *attend_back(queries, key_rows, value_matrix, weights, attn, attn_grad))

    moved, q_home, k_home, v_home = by_mask(mask, backward)
    rounded = lax.reduce_precision(spread, 8, 7)
    upper = rounded.astype(BF16)
    lower = (spread - rounded).astype(BF16)
    added = tn(jnp.concatenate([upper, lower]), jnp.concatenate([out_rows, out_rows]))
    layer = (moved.astype(F32) + added).astype(BF16)
    return (layer[None], q_home[None], k_home[None], v_home[None])


def solution(mesh):
    fine = Mesh(mesh.devices.reshape(4, 2, 4, 8), ("x", "c", "y", "z"))
    every = ("x", "c", "y", "z")
    expert = ("y", "z")
    return jax.shard_map(
        shards,
        mesh=fine,
        in_specs=(
            P(every),
            P(every),
            P(every),
            P(expert),
            P(expert),
            P(),
            P(expert),
            P(expert),
            P(expert),
            P(every),
            P(every),
            P(every),
        ),
        out_specs=(P(every), P(every), P(every), P(every)),
        check_vma=False,
    )
```

```python
import functools

import jax
import jax.numpy as jnp
from jax import lax
from jax.experimental import pallas as pl
from jax.experimental.pallas import tpu as pltpu
from jax.sharding import Mesh
from jax.sharding import PartitionSpec as P

HEAD_SIZE = 128
QUERY_HEADS = 32
KEY_VALUE_HEADS = 2
CAP = 14
ROWS = 16
EXPERTS = 4
HEADS_AT_ONCE = 4
SPAN = HEADS_AT_ONCE * HEAD_SIZE
SCALE = HEAD_SIZE ** (-0.5)
F32 = jnp.float32
BF16 = jnp.bfloat16
MIB = 1 << 20


def nt(left, right):
    return lax.dot_general(left, right, (((1,), (1,)), ((), ())), preferred_element_type=F32)


def tn(left, right):
    return lax.dot_general(left, right, (((0,), (0,)), ((), ())), preferred_element_type=F32)


def nn(left, right):
    return jnp.dot(left, right, preferred_element_type=F32)


def stacked(wide):
    return jnp.concatenate(
        [wide[:, i * HEAD_SIZE : (i + 1) * HEAD_SIZE] for i in range(HEADS_AT_ONCE)], axis=0
    )


def side_by_side(tall):
    count = tall.shape[0] // HEADS_AT_ONCE
    return jnp.concatenate(
        [tall[i * count : (i + 1) * count] for i in range(HEADS_AT_ONCE)], axis=1
    )


def allowed_keys(lengths_ref, rank_ref, count):
    rank = rank_ref[0]
    here = lax.broadcasted_iota(jnp.int32, (count, count), 0)
    there = lax.broadcasted_iota(jnp.int32, (count, count), 1)
    bound = jnp.int32(0)
    mine = jnp.zeros((count, count), jnp.int32)
    other = jnp.zeros((count, count), jnp.int32)
    for i in range(lengths_ref.shape[1]):
        bound = bound + lengths_ref[rank, i]
        mine = mine + (here >= bound).astype(jnp.int32)
        other = other + (there >= bound).astype(jnp.int32)
    allowed = (mine == other) & (there <= here)
    return jnp.concatenate([allowed.astype(jnp.int32)] * HEADS_AT_ONCE, axis=0) > 0


def softmax_rows(tall, k_part, allowed):
    scores = jnp.where(allowed, nt(tall, k_part) * SCALE, -1e30)
    expo = jnp.exp(scores - jnp.max(scores, axis=-1, keepdims=True))
    return expo / jnp.sum(expo, axis=-1, keepdims=True)


def head_part(ref, step):
    steps = QUERY_HEADS // (KEY_VALUE_HEADS * HEADS_AT_ONCE)
    return ref[:, pl.ds(pl.multiple_of(step // steps * HEAD_SIZE, HEAD_SIZE), HEAD_SIZE)]


def span_of(step):
    return pl.ds(pl.multiple_of(step * SPAN, SPAN), SPAN)


def route_kernel(
    place_ref, ids_ref, gates_ref, grad_ref, select_ref, upper_ref, lower_ref, *pair_refs
):
    count = ids_ref.shape[0]
    ids, gates = ids_ref[...], gates_ref[...]
    here = lax.broadcasted_iota(jnp.int32, (count, count), 0)
    there = lax.broadcasted_iota(jnp.int32, (count, count), 1)
    group, slot = there // ROWS, there % ROWS
    present = jnp.zeros((count, count), F32)
    weight = jnp.zeros((count, count), F32)
    for i in range(EXPERTS):
        hit = ids == lax.rem(place_ref[0] + i, EXPERTS)
        found = jnp.max(hit.astype(F32), axis=-1, keepdims=True)
        amount = jnp.sum(jnp.where(hit, gates, 0.0), axis=-1, keepdims=True)
        present = jnp.where(group == i, found, present)
        weight = jnp.where(group == i, amount, weight)
    counts = nn((there < here).astype(BF16), present.astype(BF16))
    select = (present > 0.5) & (counts == slot.astype(F32))
    chosen = select.astype(F32).astype(BF16)
    select_ref[...] = chosen
    spread = jnp.where(select, weight, 0.0)
    upper = spread.astype(BF16)
    upper_ref[...] = upper
    lower_ref[...] = (spread - upper.astype(F32)).astype(BF16)
    total = EXPERTS * ROWS
    slot_weight = jnp.sum(jnp.transpose(spread), axis=-1, keepdims=True)[:total]
    picker = jnp.transpose(select.astype(F32))[:total].astype(BF16)
    line = lax.broadcasted_iota(jnp.int32, (total, 1), 0) % ROWS
    mark = jnp.where(line == ROWS - 1, place_ref[1].astype(F32), 0.0)

    def gather(step, carry):
        rows = (slot_weight * nn(picker, grad_ref[:, span_of(step)]) + mark).astype(BF16)
        for i, pair_ref in enumerate(pair_refs):
            pair_ref[:, span_of(step)] = rows[i * ROWS : (i + 1) * ROWS]
        return carry

    lax.fori_loop(0, grad_ref.shape[1] // SPAN, gather, 0)


def forward_kernel(
    lengths_ref, rank_ref, q_ref, k_ref, v_ref, gain_ref, select_ref, attn_ref, *row_refs
):
    count, width = q_ref.shape
    allowed = allowed_keys(lengths_ref, rank_ref, count)

    def heads(step, total):
        probs = softmax_rows(stacked(q_ref[:, span_of(step)]), head_part(k_ref, step), allowed)
        mixed = side_by_side(nn(probs.astype(BF16), head_part(v_ref, step))).astype(BF16)
        attn_ref[:, span_of(step)] = mixed
        wide = mixed.astype(F32)
        return total + jnp.sum(wide * wide, axis=-1, keepdims=True)

    total = lax.fori_loop(0, width // SPAN, heads, jnp.zeros((count, 1), F32))
    scaling = lax.rsqrt(total / width + 1e-06)
    slots = EXPERTS * ROWS
    picker = jnp.transpose(select_ref[...].astype(F32))[:slots].astype(BF16)

    def norm(step, carry):
        wide = attn_ref[:, span_of(step)].astype(F32)
        normed = (wide * scaling * gain_ref[:, span_of(step)]).astype(BF16)
        rows = nn(picker, normed).astype(BF16)
        for i, row_ref in enumerate(row_refs):
            row_ref[:, span_of(step)] = rows[i * ROWS : (i + 1) * ROWS]
        return carry

    lax.fori_loop(0, width // SPAN, norm, 0)


def backward_kernel(
    lengths_ref,
    rank_ref,
    q_ref,
    k_ref,
    v_ref,
    attn_ref,
    grad_ref,
    gain_ref,
    spread_ref,
    in0_ref,
    in1_ref,
    in2_ref,
    in3_ref,
    q_out,
    k_out,
    v_out,
    normed_grad,
):
    count, width = q_ref.shape
    allowed = allowed_keys(lengths_ref, rank_ref, count)
    in_refs = (in0_ref, in1_ref, in2_ref, in3_ref)

    def gather(step, carry):
        square, product = carry
        span = span_of(step)
        rows = jnp.concatenate([ref[:, span] for ref in in_refs], axis=0)
        grad = nn(spread_ref[:, : EXPERTS * ROWS], rows)
        normed_grad[:, span] = grad
        wide = attn_ref[:, span].astype(F32)
        square = square + jnp.sum(wide * wide, axis=-1, keepdims=True)
        product = product + jnp.sum(wide * gain_ref[:, span] * grad, axis=-1, keepdims=True)
        return square, product

    zero = jnp.zeros((count, 1), F32)
    square, product = lax.fori_loop(0, width // SPAN, gather, (zero, zero))
    scaling = lax.rsqrt(square / width + 1e-06)
    lost = scaling * scaling * scaling * (product / width)
    k_sums = [jnp.zeros((count, HEAD_SIZE), F32)] * KEY_VALUE_HEADS
    v_sums = [jnp.zeros((count, HEAD_SIZE), F32)] * KEY_VALUE_HEADS
    steps = width // SPAN // KEY_VALUE_HEADS

    for head in range(KEY_VALUE_HEADS):
        part = slice(head * HEAD_SIZE, (head + 1) * HEAD_SIZE)

        def heads(turn, sums, head=head, part=part):
            span = span_of(turn + head * steps)
            k_part, v_part = k_ref[:, part], v_ref[:, part]
            wide = attn_ref[:, span].astype(F32)
            attn_grad = (
                grad_ref[:, span].astype(F32)
                + scaling * gain_ref[:, span] * normed_grad[:, span]
                - wide * lost
            ).astype(BF16)
            tall_q, tall_d = stacked(q_ref[:, span]), stacked(attn_grad)
            probs = softmax_rows(tall_q, k_part, allowed).astype(BF16)
            inner = stacked(attn_grad.astype(F32) * wide)
            inner = jnp.sum(inner, axis=-1, keepdims=True)
            score_grad = probs.astype(F32) * (nt(tall_d, v_part) - inner) * SCALE
            score_grad = score_grad.astype(BF16)
            q_out[:, span] = side_by_side(nn(score_grad, k_part)).astype(BF16)
            return sums[0] + tn(score_grad, tall_q), sums[1] + tn(probs, tall_d)

        zeros = jnp.zeros((count, HEAD_SIZE), F32)
        k_sum, v_sum = lax.fori_loop(0, steps, heads, (zeros, zeros))
        k_out[:, part] = k_sum.astype(BF16)
        v_out[:, part] = v_sum.astype(BF16)


def whole():
    return pl.BlockSpec(memory_space=pltpu.VMEM)


def scalars():
    return pl.BlockSpec(memory_space=pltpu.SMEM)


def shape(*dims, dtype=BF16):
    return jax.ShapeDtypeStruct(dims, dtype)


def route(place, ids, gates, grad):
    count, width = grad.shape
    out = pl.pallas_call(
        route_kernel,
        out_shape=[shape(count, count)] * 3 + [shape(ROWS, width)] * EXPERTS,
        in_specs=[scalars()] + [whole()] * 3,
        out_specs=[whole()] * (3 + EXPERTS),
        compiler_params=pltpu.CompilerParams(vmem_limit_bytes=16 * MIB),
        cost_estimate=pl.CostEstimate(
            flops=2 * EXPERTS * ROWS * count * width, bytes_accessed=3 * count * width, transcendentals=0
        ),
        name="route",
    )(place, ids, gates, grad)
    return *out[:3], list(out[3:])


def attend(lengths, rank, queries, key_rows, value_matrix, gain, select):
    count, width = queries.shape
    out = pl.pallas_call(
        forward_kernel,
        out_shape=[shape(count, width)] + [shape(ROWS, width)] * EXPERTS,
        in_specs=[scalars()] * 2 + [whole()] * 5,
        out_specs=[whole()] * (1 + EXPERTS),
        compiler_params=pltpu.CompilerParams(vmem_limit_bytes=24 * MIB),
        cost_estimate=pl.CostEstimate(
            flops=6 * QUERY_HEADS * count * count * HEAD_SIZE,
            bytes_accessed=6 * count * width,
            transcendentals=QUERY_HEADS * count * count,
        ),
        name="attend",
    )(lengths, rank, queries, key_rows, value_matrix, gain, select)
    return out[0], list(out[1:])


def attend_back(lengths, rank, queries, key_rows, value_matrix, attn, grad, gain, spread, in_rows):
    count, width = queries.shape
    return pl.pallas_call(
        backward_kernel,
        out_shape=[shape(count, width), shape(*key_rows.shape), shape(*key_rows.shape)],
        in_specs=[scalars()] * 2 + [whole()] * (7 + EXPERTS),
        out_specs=[whole()] * 3,
        scratch_shapes=[pltpu.VMEM((count, width), F32)],
        compiler_params=pltpu.CompilerParams(vmem_limit_bytes=32 * MIB),
        cost_estimate=pl.CostEstimate(
            flops=14 * QUERY_HEADS * count * count * HEAD_SIZE,
            bytes_accessed=10 * count * width,
            transcendentals=QUERY_HEADS * count * count,
        ),
        name="attend_back",
    )(lengths, rank, queries, key_rows, value_matrix, attn, grad, gain, spread, *in_rows)


CHUNK = 1024


def dense_kernel(*refs):
    *in_refs, out_ref = refs
    out_ref[...] = jnp.concatenate([ref[:CAP].astype(F32) for ref in in_refs], axis=0).astype(BF16)


def by_columns(kernel, name, inputs, outs, chunk=CHUNK):
    width = inputs[0].shape[1]
    return pl.pallas_call(
        kernel,
        grid=(width // chunk,),
        in_specs=[pl.BlockSpec((v.shape[0], chunk), lambda i: (0, i)) for v in inputs],
        out_specs=[pl.BlockSpec((rows, chunk), lambda i: (0, i)) for rows in outs],
        out_shape=[shape(rows, width) for rows in outs],
        compiler_params=pltpu.CompilerParams(vmem_limit_bytes=16 * MIB),
        cost_estimate=pl.CostEstimate(
            flops=0,
            bytes_accessed=2 * width * (sum(outs) + sum(v.shape[0] for v in inputs)),
            transcendentals=0,
        ),
        name=name,
    )(*inputs)


def dense_rows(blocks):
    return by_columns(dense_kernel, "dense_rows", blocks, [CAP * EXPERTS], 2 * CHUNK)[0]


def add_kernel(own_ref, far_ref, *out_refs):
    total = own_ref[...].astype(F32) + far_ref[...].astype(F32)
    each = total.shape[0] // len(out_refs)
    for i, out_ref in enumerate(out_refs):
        out_ref[...] = total[i * each : (i + 1) * each].astype(BF16)


def sum_kernel(*refs):
    in_refs, out_refs = refs[:-EXPERTS], refs[-EXPERTS:]
    total = in_refs[0][...].astype(F32)
    for ref in in_refs[1:]:
        total = total + ref[...].astype(F32)
    for i, out_ref in enumerate(out_refs):
        block = total[i * CAP : (i + 1) * CAP]
        empty = jnp.zeros((ROWS - CAP, block.shape[1]), F32)
        out_ref[...] = jnp.concatenate([block, empty], axis=0).astype(BF16)


def layer_kernel(home_ref, moved_ref, upper_ref, lower_ref, *refs):
    *in_refs, out_ref = refs
    rows = jnp.concatenate([ref[...] for ref in in_refs], axis=0)
    slots = rows.shape[0]
    added = nn(upper_ref[:, :slots], rows) + nn(lower_ref[:, :slots], rows)
    out_ref[...] = (moved_ref[0].astype(F32) + added).astype(BF16)


def layer_rows(home, moved, upper, lower, rows):
    _, count, width = moved.shape
    wide = lambda n: pl.BlockSpec((n, CHUNK), lambda i, home: (0, i))
    fixed = pl.BlockSpec(upper.shape, lambda i, home: (0, 0))
    return pl.pallas_call(
        layer_kernel,
        grid_spec=pltpu.PrefetchScalarGridSpec(
            num_scalar_prefetch=1,
            grid=(width // CHUNK,),
            in_specs=[
                pl.BlockSpec((1, count, CHUNK), lambda i, home: (home[0], 0, i)),
                fixed,
                fixed,
                *([wide(ROWS)] * EXPERTS),
            ],
            out_specs=wide(count),
        ),
        out_shape=shape(count, width),
        compiler_params=pltpu.CompilerParams(vmem_limit_bytes=58 * MIB),
        cost_estimate=pl.CostEstimate(
            flops=4 * count * width * ROWS * EXPERTS, bytes_accessed=5 * count * width, transcendentals=0
        ),
        name="layer_rows",
    )(home, moved, upper, lower, *rows)


def joined(refs):
    return jnp.concatenate([ref[...].astype(F32) for ref in refs], axis=0).astype(BF16)


def experts_in_kernel(steps, blocks, *refs):
    row_refs, grad_refs = refs[:blocks], refs[blocks : 2 * blocks]
    mats_ref, match_ref, own_ref, far_ref, hidden_ref = refs[2 * blocks : 2 * blocks + 5]
    gate_in, up_in, hidden_grad, both = refs[2 * blocks + 5 :]
    step = pl.program_id(0)
    units = mats_ref.shape[1]

    @pl.when(step == 0)
    def _():
        gate_in[...] = jnp.zeros_like(gate_in)
        up_in[...] = jnp.zeros_like(up_in)
        hidden_grad[...] = jnp.zeros_like(hidden_grad)

    @pl.when(step < steps)
    def _():
        rows = joined(row_refs)
        gate_in[...] += nt(rows, mats_ref[0])
        up_in[...] += nt(rows, mats_ref[1])
        hidden_grad[...] += nt(joined(grad_refs), mats_ref[2])

    @pl.when(step == steps - 1)
    def _():
        match = match_ref[...]
        rest = hidden_grad[...]
        grad = jnp.zeros_like(rest)
        for _ in range(3):
            piece = rest.astype(BF16)
            grad = grad + nn(match, piece)
            rest = rest - piece.astype(F32)
        gate = gate_in[...]
        up = up_in[...]
        sigma = jax.nn.sigmoid(gate)
        active = gate * sigma
        hidden_ref[...] = tn(match, (active * up).astype(BF16)).astype(BF16)
        both[:, :units] = (grad * up * sigma * (1.0 + gate * (1.0 - sigma))).astype(BF16)
        both[:, units:] = (grad * active).astype(BF16)

    @pl.when(step >= steps)
    def _():
        half = own_ref.shape[0]
        mats = jnp.concatenate([mats_ref[0], mats_ref[1]], axis=0)
        far_ref[...] = nn(both[half:], mats).astype(BF16)
        own_ref[...] = nn(both[:half], mats).astype(BF16)


def experts_in(rows, grads, mats, match):
    blocks = len(rows)
    each, width = rows[0].shape
    total = blocks * each
    units = mats.shape[1]
    steps = width // CHUNK
    half = total // 2
    first = lambda i: (0, jnp.minimum(i, steps - 1))
    last = lambda i: (0, jnp.maximum(i - steps, 0))
    fixed = lambda i: (0, 0)
    return pl.pallas_call(
        functools.partial(experts_in_kernel, steps, blocks),
        grid=(2 * steps,),
        in_specs=[
            *([pl.BlockSpec((each, CHUNK), first)] * (2 * blocks)),
            pl.BlockSpec((3, units, CHUNK), lambda i: (0, 0, lax.rem(i, steps))),
            pl.BlockSpec((total, total), fixed),
        ],
        out_specs=[
            pl.BlockSpec((half, CHUNK), last),
            pl.BlockSpec((half, CHUNK), last),
            pl.BlockSpec((total, units), fixed),
        ],
        out_shape=[shape(half, width), shape(half, width), shape(total, units)],
        scratch_shapes=[pltpu.VMEM((total, units), F32)] * 3 + [pltpu.VMEM((total, 2 * units), BF16)],
        compiler_params=pltpu.CompilerParams(vmem_limit_bytes=58 * MIB),
        cost_estimate=pl.CostEstimate(
            flops=10 * total * width * units, bytes_accessed=6 * total * width + 12 * units * width,
            transcendentals=total * units,
        ),
        name="experts_in",
    )(*rows, *grads, mats, match)


def experts_out_kernel(hidden_ref, mats_ref, own_ref, far_ref):
    half = own_ref.shape[0]
    far_ref[...] = nn(hidden_ref[half:], mats_ref[0]).astype(BF16)
    own_ref[...] = nn(hidden_ref[:half], mats_ref[0]).astype(BF16)


def experts_out(hidden, mats):
    total, units = hidden.shape
    width = mats.shape[2]
    half = total // 2
    return pl.pallas_call(
        experts_out_kernel,
        grid=(width // CHUNK,),
        in_specs=[
            pl.BlockSpec((total, units), lambda i: (0, 0)),
            pl.BlockSpec((1, units, CHUNK), lambda i: (2, 0, i)),
        ],
        out_specs=[pl.BlockSpec((half, CHUNK), lambda i: (0, i))] * 2,
        out_shape=[shape(half, width)] * 2,
        compiler_params=pltpu.CompilerParams(vmem_limit_bytes=16 * MIB),
        cost_estimate=pl.CostEstimate(
            flops=2 * total * width * units, bytes_accessed=2 * total * width + 2 * units * width,
            transcendentals=0,
        ),
        name="experts_out",
    )(hidden, mats)


def shifted(value, axis, step):
    size = lax.axis_size(axis)
    if step % size == 0:
        return value
    return lax.ppermute(value, axis, [(i, (i + step) % size) for i in range(size)])


def swapped(value):
    return lax.ppermute(value, "c", [(0, 1), (1, 0)])


def to_experts(blocks):
    return [shifted(blocks[s], "y", s) for s in range(EXPERTS)]


def from_experts(blocks):
    return [shifted(blocks[s], "y", -s) for s in range(EXPERTS)]


def gather_rows(block):
    mine = [shifted(block, "x", s) for s in range(lax.axis_size("x"))]
    return mine + [swapped(b) for b in mine]


def add_far(own, far):
    size = lax.axis_size("x")
    return by_columns(add_kernel, "add_rows", [own, swapped(far)], [own.shape[0] // size] * size)


def scatter_sums(blocks):
    parts = [shifted(b, "x", -s) for s, b in enumerate(blocks)]
    return by_columns(sum_kernel, "sum_rows", parts, [ROWS] * EXPERTS)


def by_mask(mask, *values):
    ranks = lax.axis_size("x") * lax.axis_size("c")

    def branch(k):
        pairs = [(i, i ^ k) for i in range(ranks)]
        return lambda *v: tuple(lax.ppermute(one, ("x", "c"), pairs) for one in v)

    return lax.switch(mask - 1, [branch(k) for k in range(1, ranks)], *values)


def after(values, other):
    return lax.optimization_barrier((values, other))[0]


def shards(
    queries,
    key_rows,
    value_matrix,
    doc_lengths,
    seq_plan,
    norm_gain,
    w_gate,
    w_up,
    w_down,
    expert_ids,
    gate_weights,
    out_grad,
):
    queries, key_rows, value_matrix, out_grad = queries[0], key_rows[0], value_matrix[0], out_grad[0]
    w_gate, w_up, w_down = w_gate[0], w_up[0], w_down[0]
    route_ids, route_gates = expert_ids[0], gate_weights[0]
    x, c, y = lax.axis_index("x"), lax.axis_index("c"), lax.axis_index("y")
    x_size = lax.axis_size("x")
    ranks = 2 * x_size
    rank = x * 2 + c
    count, width = queries.shape
    mask = seq_plan[0, 0]
    gain = norm_gain[None]
    lengths = doc_lengths[0]
    rank_word = jnp.full((1,), rank, jnp.int32)

    units = w_gate.shape[1] // ranks
    pieces = jnp.stack(
        [
            lax.dynamic_slice_in_dim(m, rank * units, units, 0)
            for m in (jnp.transpose(w_gate), jnp.transpose(w_up), w_down)
        ]
    )
    mats = lax.all_gather(pieces, "z", axis=1, tiled=True)

    place = jnp.stack([y, mask]).astype(jnp.int32)
    select, upper, lower, pair_blocks = route(
        *after((place, route_ids, route_gates, out_grad), pieces)
    )
    pair_blocks = to_experts(pair_blocks)
    masks = jnp.stack([v[ROWS - 1, 0] for v in pair_blocks]).astype(jnp.int32)
    select_home, grad_home = by_mask(mask, select, out_grad)
    pair_block = dense_rows(pair_blocks)
    queries, grad_home = after((queries, grad_home), pair_block)
    attn, row_blocks = attend(
        lengths, rank_word, queries, key_rows, value_matrix, gain, select_home
    )
    grads = gather_rows(pair_block)
    row_block = dense_rows(to_experts(row_blocks))
    rows = gather_rows(row_block)
    moved = lax.all_gather(attn, ("x", "c"))

    index = jnp.arange(2 * x_size * EXPERTS * CAP, dtype=jnp.int32)
    turn = (index // CAP) % EXPERTS
    away = (index // (CAP * EXPERTS)) % x_size
    flip = index // (CAP * EXPERTS * x_size)
    owner = ((x - away) % x_size) * 2 + (c ^ flip)
    tail = turn * CAP + index % CAP
    slot_key = owner * (EXPERTS * CAP) + tail
    masks_of = jnp.sum(
        jnp.where(turn[:, None] == jnp.arange(EXPERTS)[None, :], masks[None, :], 0), axis=1
    )
    home_key = (owner ^ masks_of) * (EXPERTS * CAP) + tail
    match = (home_key[:, None] == slot_key[None, :]).astype(BF16)

    own_in, far_in, hidden = experts_in(rows, grads, mats, match)
    own_out, far_out = experts_out(hidden, mats)
    in_blocks = add_far(own_in, far_in)
    out_blocks = add_far(*after((own_out, far_out), in_blocks))
    in_sums = scatter_sums(in_blocks)
    in_rows = from_experts(in_sums)
    out_sums = scatter_sums([after(out_blocks[0], in_sums[0]), *out_blocks[1:]])
    out_rows = from_experts(out_sums)
    in_rows = after(in_rows, out_sums)

    q_home, k_home, v_home = attend_back(
        lengths, rank_word, queries, key_rows, value_matrix, attn, grad_home, gain,
        select_home, in_rows,
    )
    layer = layer_rows(rank_word ^ mask, moved, after(upper, k_home), lower, out_rows)
    return (layer[None], q_home[None], k_home[None], v_home[None])


def solution(mesh):
    fine = Mesh(mesh.devices.reshape(4, 2, 4, 8), ("x", "c", "y", "z"))
    every = ("x", "c", "y", "z")
    expert = ("y", "z")
    return jax.shard_map(
        shards,
        mesh=fine,
        in_specs=(
            P(every),
            P(every),
            P(every),
            P(expert),
            P(expert),
            P(),
            P(expert),
            P(expert),
            P(expert),
            P(every),
            P(every),
            P(every),
        ),
        out_specs=(P(every), P(every), P(every), P(every)),
        check_vma=False,
    )
```

```python
import functools

import jax
import jax.numpy as jnp
from jax import lax
from jax.experimental import pallas as pl
from jax.experimental.pallas import tpu as pltpu
from jax.sharding import Mesh
from jax.sharding import PartitionSpec as P

HEAD_SIZE = 128
QUERY_HEADS = 32
KEY_VALUE_HEADS = 2
CAP = 14
ROWS = 16
EXPERTS = 4
HEADS_AT_ONCE = 4
SPAN = HEADS_AT_ONCE * HEAD_SIZE
SCALE = HEAD_SIZE ** (-0.5)
F32 = jnp.float32
BF16 = jnp.bfloat16
MIB = 1 << 20


def nt(left, right):
    return lax.dot_general(left, right, (((1,), (1,)), ((), ())), preferred_element_type=F32)


def tn(left, right):
    return lax.dot_general(left, right, (((0,), (0,)), ((), ())), preferred_element_type=F32)


def nn(left, right):
    return jnp.dot(left, right, preferred_element_type=F32)


def stacked(wide):
    return jnp.concatenate(
        [wide[:, i * HEAD_SIZE : (i + 1) * HEAD_SIZE] for i in range(HEADS_AT_ONCE)], axis=0
    )


def side_by_side(tall):
    count = tall.shape[0] // HEADS_AT_ONCE
    return jnp.concatenate(
        [tall[i * count : (i + 1) * count] for i in range(HEADS_AT_ONCE)], axis=1
    )


def allowed_keys(lengths_ref, rank_ref, count):
    rank = rank_ref[0]
    here = lax.broadcasted_iota(jnp.int32, (count, count), 0)
    there = lax.broadcasted_iota(jnp.int32, (count, count), 1)
    bound = jnp.int32(0)
    mine = jnp.zeros((count, count), jnp.int32)
    other = jnp.zeros((count, count), jnp.int32)
    for i in range(lengths_ref.shape[1]):
        bound = bound + lengths_ref[rank, i]
        mine = mine + (here >= bound).astype(jnp.int32)
        other = other + (there >= bound).astype(jnp.int32)
    allowed = (mine == other) & (there <= here)
    return jnp.concatenate([allowed.astype(jnp.int32)] * HEADS_AT_ONCE, axis=0) > 0


def softmax_rows(tall, k_part, allowed):
    scores = jnp.where(allowed, nt(tall, k_part) * SCALE, -1e30)
    expo = jnp.exp(scores - jnp.max(scores, axis=-1, keepdims=True))
    return expo / jnp.sum(expo, axis=-1, keepdims=True)


def head_part(ref, step):
    steps = QUERY_HEADS // (KEY_VALUE_HEADS * HEADS_AT_ONCE)
    return ref[:, pl.ds(pl.multiple_of(step // steps * HEAD_SIZE, HEAD_SIZE), HEAD_SIZE)]


def span_of(step):
    return pl.ds(pl.multiple_of(step * SPAN, SPAN), SPAN)


def route_kernel(
    place_ref, ids_ref, gates_ref, grad_ref, select_ref, upper_ref, lower_ref, *pair_refs
):
    count = ids_ref.shape[0]
    ids, gates = ids_ref[...], gates_ref[...]
    here = lax.broadcasted_iota(jnp.int32, (count, count), 0)
    there = lax.broadcasted_iota(jnp.int32, (count, count), 1)
    group, slot = there // ROWS, there % ROWS
    present = jnp.zeros((count, count), F32)
    weight = jnp.zeros((count, count), F32)
    for i in range(EXPERTS):
        hit = ids == lax.rem(place_ref[0] + i, EXPERTS)
        found = jnp.max(hit.astype(F32), axis=-1, keepdims=True)
        amount = jnp.sum(jnp.where(hit, gates, 0.0), axis=-1, keepdims=True)
        present = jnp.where(group == i, found, present)
        weight = jnp.where(group == i, amount, weight)
    counts = nn((there < here).astype(BF16), present.astype(BF16))
    select = (present > 0.5) & (counts == slot.astype(F32))
    chosen = select.astype(F32).astype(BF16)
    select_ref[...] = chosen
    spread = jnp.where(select, weight, 0.0)
    upper = spread.astype(BF16)
    upper_ref[...] = upper
    lower_ref[...] = (spread - upper.astype(F32)).astype(BF16)
    total = EXPERTS * ROWS
    slot_weight = jnp.sum(jnp.transpose(spread), axis=-1, keepdims=True)[:total]
    picker = jnp.transpose(select.astype(F32))[:total].astype(BF16)
    line = lax.broadcasted_iota(jnp.int32, (total, 1), 0) % ROWS
    mark = jnp.where(line == ROWS - 1, place_ref[1].astype(F32), 0.0)

    def gather(step, carry):
        rows = (slot_weight * nn(picker, grad_ref[:, span_of(step)]) + mark).astype(BF16)
        for i, pair_ref in enumerate(pair_refs):
            pair_ref[:, span_of(step)] = rows[i * ROWS : (i + 1) * ROWS]
        return carry

    lax.fori_loop(0, grad_ref.shape[1] // SPAN, gather, 0)


def forward_kernel(
    lengths_ref, rank_ref, q_ref, k_ref, v_ref, gain_ref, select_ref, attn_ref, probs_ref, *row_refs
):
    count, width = q_ref.shape
    allowed = allowed_keys(lengths_ref, rank_ref, count)

    def heads(step, total):
        probs = softmax_rows(stacked(q_ref[:, span_of(step)]), head_part(k_ref, step), allowed)
        probs = probs.astype(BF16)
        probs_ref[step] = probs
        mixed = side_by_side(nn(probs, head_part(v_ref, step))).astype(BF16)
        attn_ref[:, span_of(step)] = mixed
        wide = mixed.astype(F32)
        return total + jnp.sum(wide * wide, axis=-1, keepdims=True)

    total = lax.fori_loop(0, width // SPAN, heads, jnp.zeros((count, 1), F32))
    scaling = lax.rsqrt(total / width + 1e-06)
    slots = EXPERTS * ROWS
    picker = jnp.transpose(select_ref[...].astype(F32))[:slots].astype(BF16)

    def norm(step, carry):
        wide = attn_ref[:, span_of(step)].astype(F32)
        normed = (wide * scaling * gain_ref[:, span_of(step)]).astype(BF16)
        rows = nn(picker, normed).astype(BF16)
        for i, row_ref in enumerate(row_refs):
            row_ref[:, span_of(step)] = rows[i * ROWS : (i + 1) * ROWS]
        return carry

    lax.fori_loop(0, width // SPAN, norm, 0)


def backward_kernel(
    probs_ref,
    q_ref,
    k_ref,
    v_ref,
    attn_ref,
    grad_ref,
    gain_ref,
    spread_ref,
    in0_ref,
    in1_ref,
    in2_ref,
    in3_ref,
    q_out,
    k_out,
    v_out,
    normed_grad,
):
    count, width = q_ref.shape
    in_refs = (in0_ref, in1_ref, in2_ref, in3_ref)

    def gather(step, carry):
        square, product = carry
        span = span_of(step)
        rows = jnp.concatenate([ref[:, span] for ref in in_refs], axis=0)
        grad = nn(spread_ref[:, : EXPERTS * ROWS], rows)
        normed_grad[:, span] = grad
        wide = attn_ref[:, span].astype(F32)
        square = square + jnp.sum(wide * wide, axis=-1, keepdims=True)
        product = product + jnp.sum(wide * gain_ref[:, span] * grad, axis=-1, keepdims=True)
        return square, product

    zero = jnp.zeros((count, 1), F32)
    square, product = lax.fori_loop(0, width // SPAN, gather, (zero, zero))
    scaling = lax.rsqrt(square / width + 1e-06)
    lost = scaling * scaling * scaling * (product / width)
    k_sums = [jnp.zeros((count, HEAD_SIZE), F32)] * KEY_VALUE_HEADS
    v_sums = [jnp.zeros((count, HEAD_SIZE), F32)] * KEY_VALUE_HEADS
    steps = width // SPAN // KEY_VALUE_HEADS

    for head in range(KEY_VALUE_HEADS):
        part = slice(head * HEAD_SIZE, (head + 1) * HEAD_SIZE)

        def heads(turn, sums, head=head, part=part):
            step = turn + head * steps
            span = span_of(step)
            k_part, v_part = k_ref[:, part], v_ref[:, part]
            wide = attn_ref[:, span].astype(F32)
            attn_grad = (
                grad_ref[:, span].astype(F32)
                + scaling * gain_ref[:, span] * normed_grad[:, span]
                - wide * lost
            ).astype(BF16)
            tall_q, tall_d = stacked(q_ref[:, span]), stacked(attn_grad)
            probs = probs_ref[step]
            inner = stacked(attn_grad.astype(F32) * wide)
            inner = jnp.sum(inner, axis=-1, keepdims=True)
            score_grad = probs.astype(F32) * (nt(tall_d, v_part) - inner) * SCALE
            score_grad = score_grad.astype(BF16)
            q_out[:, span] = side_by_side(nn(score_grad, k_part)).astype(BF16)
            return sums[0] + tn(score_grad, tall_q), sums[1] + tn(probs, tall_d)

        zeros = jnp.zeros((count, HEAD_SIZE), F32)
        k_sum, v_sum = lax.fori_loop(0, steps, heads, (zeros, zeros))
        k_out[:, part] = k_sum.astype(BF16)
        v_out[:, part] = v_sum.astype(BF16)


def cost(micros):
    return pl.CostEstimate(
        flops=int(micros * 1.15e9), bytes_accessed=int(micros * 3.6e6), transcendentals=0
    )


def whole():
    return pl.BlockSpec(memory_space=pltpu.VMEM)


def scalars():
    return pl.BlockSpec(memory_space=pltpu.SMEM)


def shape(*dims, dtype=BF16):
    return jax.ShapeDtypeStruct(dims, dtype)


def route(place, ids, gates, grad):
    count, width = grad.shape
    out = pl.pallas_call(
        route_kernel,
        out_shape=[shape(count, count)] * 3 + [shape(ROWS, width)] * EXPERTS,
        in_specs=[scalars()] + [whole()] * 3,
        out_specs=[whole()] * (3 + EXPERTS),
        compiler_params=pltpu.CompilerParams(vmem_limit_bytes=16 * MIB),
        cost_estimate=cost(3.5),
        name="route",
    )(place, ids, gates, grad)
    return *out[:3], list(out[3:])


def attend(lengths, rank, queries, key_rows, value_matrix, gain, select):
    count, width = queries.shape
    out = pl.pallas_call(
        forward_kernel,
        out_shape=[
            shape(count, width),
            shape(QUERY_HEADS // HEADS_AT_ONCE, HEADS_AT_ONCE * count, count),
            *([shape(ROWS, width)] * EXPERTS),
        ],
        in_specs=[scalars()] * 2 + [whole()] * 5,
        out_specs=[whole()] * (2 + EXPERTS),
        compiler_params=pltpu.CompilerParams(vmem_limit_bytes=24 * MIB),
        cost_estimate=cost(8.2),
        name="attend",
    )(lengths, rank, queries, key_rows, value_matrix, gain, select)
    return out[0], out[1], list(out[2:])


def attend_back(probs, queries, key_rows, value_matrix, attn, grad, gain, spread, in_rows):
    count, width = queries.shape
    return pl.pallas_call(
        backward_kernel,
        out_shape=[shape(count, width), shape(*key_rows.shape), shape(*key_rows.shape)],
        in_specs=[whole()] * (8 + EXPERTS),
        out_specs=[whole()] * 3,
        scratch_shapes=[pltpu.VMEM((count, width), F32)],
        compiler_params=pltpu.CompilerParams(vmem_limit_bytes=32 * MIB),
        cost_estimate=cost(9.8),
        name="attend_back",
    )(probs, queries, key_rows, value_matrix, attn, grad, gain, spread, *in_rows)


CHUNK = 1024


def dense_kernel(*refs):
    *in_refs, out_ref = refs
    out_ref[...] = jnp.concatenate([ref[:CAP].astype(F32) for ref in in_refs], axis=0).astype(BF16)


def by_columns(kernel, name, inputs, outs, chunk=CHUNK):
    width = inputs[0].shape[1]
    return pl.pallas_call(
        kernel,
        grid=(width // chunk,),
        in_specs=[pl.BlockSpec((v.shape[0], chunk), lambda i: (0, i)) for v in inputs],
        out_specs=[pl.BlockSpec((rows, chunk), lambda i: (0, i)) for rows in outs],
        out_shape=[shape(rows, width) for rows in outs],
        compiler_params=pltpu.CompilerParams(vmem_limit_bytes=16 * MIB),
        cost_estimate=pl.CostEstimate(
            flops=0,
            bytes_accessed=2 * width * (sum(outs) + sum(v.shape[0] for v in inputs)),
            transcendentals=0,
        ),
        name=name,
    )(*inputs)


def dense_rows(blocks):
    return by_columns(dense_kernel, "dense_rows", blocks, [CAP * EXPERTS], 2 * CHUNK)[0]


def add_kernel(own_ref, far_ref, *out_refs):
    total = own_ref[...].astype(F32) + far_ref[...].astype(F32)
    start = 0
    for out_ref in out_refs:
        out_ref[...] = total[start : start + out_ref.shape[0]].astype(BF16)
        start += out_ref.shape[0]


def relay_kernel(left_ref, right_ref, top_ref, low_ref, left_out, right_out):
    left, right = left_ref[...].astype(F32), right_ref[...].astype(F32)
    top = top_ref.shape[0]
    left_out[...] = jnp.concatenate(
        [left[:top] + top_ref[...].astype(F32), left[top:]], axis=0
    ).astype(BF16)
    right_out[...] = jnp.concatenate(
        [right[:top], right[top:] + low_ref[...].astype(F32)], axis=0
    ).astype(BF16)


def sum_kernel(*refs):
    in_refs, out_refs = refs[:-EXPERTS], refs[-EXPERTS:]
    total = in_refs[0][...].astype(F32)
    for ref in in_refs[1:]:
        total = total + ref[...].astype(F32)
    for i, out_ref in enumerate(out_refs):
        block = total[i * CAP : (i + 1) * CAP]
        empty = jnp.zeros((ROWS - CAP, block.shape[1]), F32)
        out_ref[...] = jnp.concatenate([block, empty], axis=0).astype(BF16)


def match_kernel(place_ref, *refs):
    *mark_refs, out_ref = refs
    total = out_ref.shape[0]
    size = total // (2 * CAP * EXPERTS)

    def keys(dims, axis, marked):
        index = lax.broadcasted_iota(jnp.int32, dims, axis)
        block, turn = index // (CAP * EXPERTS), index // CAP % EXPERTS
        away, flip = block % size, block // size
        owner = (place_ref[0] + size - away) % size * 2 + (place_ref[1] ^ flip)
        if marked:
            mask = jnp.zeros(dims, jnp.int32)
            for i, ref in enumerate(mark_refs):
                mark = ref[ROWS - 1 :, :1].astype(F32).astype(jnp.int32)
                mask = jnp.where(turn == i, mark, mask)
            owner = owner ^ mask
        return owner * (CAP * EXPERTS) + index % (CAP * EXPERTS)

    same = keys((total, 1), 0, True) == keys((1, total), 1, False)
    out_ref[...] = same.astype(F32).astype(BF16)


def match_of(place, blocks, devices):
    total = devices * CAP * EXPERTS
    return pl.pallas_call(
        match_kernel,
        grid=(1,),
        in_specs=[
            pl.BlockSpec(memory_space=pltpu.SMEM),
            *([pl.BlockSpec((ROWS, HEAD_SIZE), lambda i: (0, 0))] * len(blocks)),
        ],
        out_specs=pl.BlockSpec((total, total), lambda i: (0, 0)),
        out_shape=shape(total, total),
        compiler_params=pltpu.CompilerParams(vmem_limit_bytes=16 * MIB),
        cost_estimate=cost(1),
        name="match",
    )(place, *blocks)


def layer_kernel(home_ref, moved_ref, upper_ref, lower_ref, *refs):
    *in_refs, out_ref = refs
    rows = jnp.concatenate([ref[...] for ref in in_refs], axis=0)
    slots = rows.shape[0]
    added = nn(upper_ref[:, :slots], rows) + nn(lower_ref[:, :slots], rows)
    out_ref[...] = (moved_ref[0].astype(F32) + added).astype(BF16)


def layer_rows(home, moved, upper, lower, rows):
    _, count, width = moved.shape
    wide = lambda n: pl.BlockSpec((n, CHUNK), lambda i, home: (0, i))
    fixed = pl.BlockSpec(upper.shape, lambda i, home: (0, 0))
    return pl.pallas_call(
        layer_kernel,
        grid_spec=pltpu.PrefetchScalarGridSpec(
            num_scalar_prefetch=1,
            grid=(width // CHUNK,),
            in_specs=[
                pl.BlockSpec((1, count, CHUNK), lambda i, home: (home[0], 0, i)),
                fixed,
                fixed,
                *([wide(ROWS)] * EXPERTS),
            ],
            out_specs=wide(count),
        ),
        out_shape=shape(count, width),
        compiler_params=pltpu.CompilerParams(vmem_limit_bytes=58 * MIB),
        cost_estimate=cost(4),
        name="layer_rows",
    )(home, moved, upper, lower, *rows)


def joined(refs):
    return jnp.concatenate([ref[...].astype(F32) for ref in refs], axis=0).astype(BF16)


def hidden_grad_kernel(*refs):
    *grad_refs, mats_ref, out_ref = refs

    @pl.when(pl.program_id(0) == 0)
    def _():
        out_ref[...] = jnp.zeros_like(out_ref)

    out_ref[...] += nt(joined(grad_refs), mats_ref[0])


def hidden_grad_of(grads, mats):
    each, width = grads[0].shape
    total, units = len(grads) * each, mats.shape[1]
    return pl.pallas_call(
        hidden_grad_kernel,
        grid=(width // CHUNK,),
        in_specs=[
            *([pl.BlockSpec((each, CHUNK), lambda i: (0, i))] * len(grads)),
            pl.BlockSpec((1, units, CHUNK), lambda i: (2, 0, i)),
        ],
        out_specs=pl.BlockSpec((total, units), lambda i: (0, 0)),
        out_shape=shape(total, units, dtype=F32),
        compiler_params=pltpu.CompilerParams(vmem_limit_bytes=58 * MIB),
        cost_estimate=cost(4),
        name="hidden_grad",
    )(*grads, mats)


def experts_in_kernel(steps, blocks, *refs):
    row_refs = refs[:blocks]
    mats_ref, match_ref, hidden_grad, own_ref, far_ref, hidden_ref = refs[blocks : blocks + 6]
    gate_in, up_in, both = refs[blocks + 6 :]
    step = pl.program_id(0)
    units = mats_ref.shape[1]

    @pl.when(step == 0)
    def _():
        gate_in[...] = jnp.zeros_like(gate_in)
        up_in[...] = jnp.zeros_like(up_in)

    @pl.when(step < steps)
    def _():
        rows = joined(row_refs)
        gate_in[...] += nt(rows, mats_ref[0])
        up_in[...] += nt(rows, mats_ref[1])

    @pl.when(step == steps - 1)
    def _():
        match = match_ref[...]
        rest = hidden_grad[...]
        grad = jnp.zeros_like(rest)
        for _ in range(3):
            piece = rest.astype(BF16)
            grad = grad + nn(match, piece)
            rest = rest - piece.astype(F32)
        gate = gate_in[...]
        up = up_in[...]
        sigma = jax.nn.sigmoid(gate)
        active = gate * sigma
        hidden_ref[...] = tn(match, (active * up).astype(BF16)).astype(BF16)
        both[:, :units] = (grad * up * sigma * (1.0 + gate * (1.0 - sigma))).astype(BF16)
        both[:, units:] = (grad * active).astype(BF16)

    @pl.when(step >= steps)
    def _():
        half = own_ref.shape[0]
        mats = jnp.concatenate([mats_ref[0], mats_ref[1]], axis=0)
        far_ref[...] = nn(both[half:], mats).astype(BF16)
        own_ref[...] = nn(both[:half], mats).astype(BF16)


def experts_in(rows, mats, match, hidden_grad):
    blocks = len(rows)
    each, width = rows[0].shape
    total = blocks * each
    units = mats.shape[1]
    steps = width // CHUNK
    half = total // 2
    first = lambda i: (0, jnp.minimum(i, steps - 1))
    last = lambda i: (0, jnp.maximum(i - steps, 0))
    fixed = lambda i: (0, 0)
    return pl.pallas_call(
        functools.partial(experts_in_kernel, steps, blocks),
        grid=(2 * steps,),
        in_specs=[
            *([pl.BlockSpec((each, CHUNK), first)] * blocks),
            pl.BlockSpec((2, units, CHUNK), lambda i: (0, 0, lax.rem(i, steps))),
            pl.BlockSpec((total, total), fixed),
            pl.BlockSpec((total, units), fixed),
        ],
        out_specs=[
            pl.BlockSpec((half, CHUNK), last),
            pl.BlockSpec((half, CHUNK), last),
            pl.BlockSpec((total, units), fixed),
        ],
        out_shape=[shape(half, width), shape(half, width), shape(total, units)],
        scratch_shapes=[pltpu.VMEM((total, units), F32)] * 2 + [pltpu.VMEM((total, 2 * units), BF16)],
        compiler_params=pltpu.CompilerParams(vmem_limit_bytes=58 * MIB),
        cost_estimate=cost(10),
        name="experts_in",
    )(*rows, mats, match, hidden_grad)


def experts_out_kernel(hidden_ref, mats_ref, own_ref, far_ref):
    half = own_ref.shape[0]
    far_ref[...] = nn(hidden_ref[half:], mats_ref[0]).astype(BF16)
    own_ref[...] = nn(hidden_ref[:half], mats_ref[0]).astype(BF16)


def experts_out(hidden, mats):
    total, units = hidden.shape
    width = mats.shape[2]
    half = total // 2
    return pl.pallas_call(
        experts_out_kernel,
        grid=(width // CHUNK,),
        in_specs=[
            pl.BlockSpec((total, units), lambda i: (0, 0)),
            pl.BlockSpec((1, units, CHUNK), lambda i: (2, 0, i)),
        ],
        out_specs=[pl.BlockSpec((half, CHUNK), lambda i: (0, i))] * 2,
        out_shape=[shape(half, width)] * 2,
        compiler_params=pltpu.CompilerParams(vmem_limit_bytes=58 * MIB),
        cost_estimate=cost(2),
        name="experts_out",
    )(hidden, mats)


def shifted(value, axis, step):
    size = lax.axis_size(axis)
    if step % size == 0:
        return value
    return lax.ppermute(value, axis, [(i, (i + step) % size) for i in range(size)])


def swapped(value):
    return lax.ppermute(value, "c", [(0, 1), (1, 0)])


def to_experts(blocks):
    return [shifted(blocks[s], "y", s) for s in range(EXPERTS)]


def from_experts(blocks):
    return [shifted(blocks[s], "y", -s) for s in range(EXPERTS)]


def along_x(block):
    return [shifted(block, "x", s) for s in range(lax.axis_size("x"))]


def both_cores(blocks):
    return blocks + [swapped(b) for b in blocks]


TOP = 32


def add_far(own, far):
    each = own.shape[0] // lax.axis_size("x")
    sizes = [each, each, TOP, each - TOP, each]
    return by_columns(add_kernel, "add_rows", [own, swapped(far)], sizes)


def half_way(blocks):
    mine, left, top, low, right = blocks
    parts = [left, right, shifted(top, "x", -1), shifted(low, "x", 1)]
    left, right = by_columns(relay_kernel, "relay_rows", parts, [left.shape[0]] * 2)
    return [mine, shifted(left, "x", -1), shifted(right, "x", 1)]


def total_of(parts):
    return by_columns(sum_kernel, "sum_rows", parts, [ROWS] * EXPERTS)


def by_mask(mask, *values):
    ranks = lax.axis_size("x") * lax.axis_size("c")

    def branch(k):
        pairs = [(i, i ^ k) for i in range(ranks)]
        return lambda *v: tuple(lax.ppermute(one, ("x", "c"), pairs) for one in v)

    return lax.switch(mask - 1, [branch(k) for k in range(1, ranks)], *values)


def after(values, other):
    return lax.optimization_barrier((values, other))[0]


def shards(
    queries,
    key_rows,
    value_matrix,
    doc_lengths,
    seq_plan,
    norm_gain,
    w_gate,
    w_up,
    w_down,
    expert_ids,
    gate_weights,
    out_grad,
):
    queries, key_rows, value_matrix, out_grad = queries[0], key_rows[0], value_matrix[0], out_grad[0]
    w_gate, w_up, w_down = w_gate[0], w_up[0], w_down[0]
    route_ids, route_gates = expert_ids[0], gate_weights[0]
    x, c, y = lax.axis_index("x"), lax.axis_index("c"), lax.axis_index("y")
    x_size = lax.axis_size("x")
    ranks = 2 * x_size
    rank = x * 2 + c
    count, width = queries.shape
    mask = seq_plan[0, 0]
    gain = norm_gain[None]
    lengths = doc_lengths[0]
    rank_word = jnp.full((1,), rank, jnp.int32)

    units = w_gate.shape[1] // ranks
    pieces = jnp.stack(
        [
            lax.dynamic_slice_in_dim(m, rank * units, units, 0)
            for m in (jnp.transpose(w_gate), jnp.transpose(w_up), w_down)
        ]
    )
    mats = lax.all_gather(pieces, "z", axis=1, tiled=True)

    place = jnp.stack([y, mask]).astype(jnp.int32)
    select, upper, lower, pair_blocks = route(
        *after((place, route_ids, route_gates, out_grad), pieces)
    )
    pair_blocks = to_experts(pair_blocks)
    (select_home,) = by_mask(mask, select)
    pair_block = dense_rows(pair_blocks)
    queries, select_home = after((queries, select_home), pair_block)
    attn, probs, row_blocks = attend(
        lengths, rank_word, queries, key_rows, value_matrix, gain, select_home
    )
    pairs_x = along_x(pair_block)
    out_grad, pairs_x = lax.optimization_barrier((after(out_grad, row_blocks[0]), pairs_x))
    row_blocks = to_experts(row_blocks)
    (grad_home,) = by_mask(mask, out_grad)
    row_block = dense_rows(after(row_blocks, grad_home))
    grads = both_cores(pairs_x)
    hidden_grad = hidden_grad_of(grads, mats)
    rows_x, hidden_grad = lax.optimization_barrier((along_x(row_block), hidden_grad))
    rows = both_cores(rows_x)
    moved = lax.all_gather(after(attn, row_block), ("x", "c"))

    match = match_of(jnp.stack([x, c]).astype(jnp.int32), pair_blocks, 2 * x_size)
    own_in, far_in, hidden = experts_in(rows, mats, match, hidden_grad)
    own_out, far_out = experts_out(hidden, mats)
    in_blocks = add_far(own_in, far_in)
    out_blocks = add_far(*after((own_out, far_out), in_blocks))
    in_parts = half_way(in_blocks)
    out_parts = half_way(out_blocks)
    in_sums = total_of(in_parts)
    in_rows = from_experts(in_sums)
    out_sums = total_of([after(out_parts[0], in_sums[0]), *out_parts[1:]])
    out_rows = from_experts(out_sums)
    in_rows = after(in_rows, out_sums)

    q_home, k_home, v_home = attend_back(
        probs, queries, key_rows, value_matrix, attn, grad_home, gain, select_home, in_rows
    )
    layer = layer_rows(rank_word ^ mask, moved, after(upper, k_home), lower, out_rows)
    return (layer[None], q_home[None], k_home[None], v_home[None])


def solution(mesh):
    fine = Mesh(mesh.devices.reshape(4, 2, 4, 8), ("x", "c", "y", "z"))
    every = ("x", "c", "y", "z")
    expert = ("y", "z")
    return jax.shard_map(
        shards,
        mesh=fine,
        in_specs=(
            P(every),
            P(every),
            P(every),
            P(expert),
            P(expert),
            P(),
            P(expert),
            P(expert),
            P(expert),
            P(every),
            P(every),
            P(every),
        ),
        out_specs=(P(every), P(every), P(every), P(every)),
        check_vma=False,
    )
```

```python
import functools

import jax
import jax.numpy as jnp
from jax import lax
from jax.experimental import pallas as pl
from jax.experimental.pallas import tpu as pltpu
from jax.sharding import Mesh
from jax.sharding import PartitionSpec as P

HEAD_SIZE = 128
QUERY_HEADS = 32
KEY_VALUE_HEADS = 2
CAP = 14
ROWS = 16
EXPERTS = 4
HEADS_AT_ONCE = 16
SPAN = HEADS_AT_ONCE * HEAD_SIZE
SCALE = HEAD_SIZE ** (-0.5)
F32 = jnp.float32
BF16 = jnp.bfloat16
MIB = 1 << 20


def nt(left, right):
    return lax.dot_general(left, right, (((1,), (1,)), ((), ())), preferred_element_type=F32)


def tn(left, right):
    return lax.dot_general(left, right, (((0,), (0,)), ((), ())), preferred_element_type=F32)


def nn(left, right):
    return jnp.dot(left, right, preferred_element_type=F32)


def stacked(wide):
    return jnp.concatenate(
        [wide[:, i * HEAD_SIZE : (i + 1) * HEAD_SIZE] for i in range(HEADS_AT_ONCE)], axis=0
    )


def side_by_side(tall):
    count = tall.shape[0] // HEADS_AT_ONCE
    return jnp.concatenate(
        [tall[i * count : (i + 1) * count] for i in range(HEADS_AT_ONCE)], axis=1
    )


def allowed_keys(lengths_ref, rank_ref, count):
    rank = rank_ref[0]
    here = lax.broadcasted_iota(jnp.int32, (count, count), 0)
    there = lax.broadcasted_iota(jnp.int32, (count, count), 1)
    bound = jnp.int32(0)
    mine = jnp.zeros((count, count), jnp.int32)
    other = jnp.zeros((count, count), jnp.int32)
    for i in range(lengths_ref.shape[1]):
        bound = bound + lengths_ref[rank, i]
        mine = mine + (here >= bound).astype(jnp.int32)
        other = other + (there >= bound).astype(jnp.int32)
    allowed = (mine == other) & (there <= here)
    return jnp.concatenate([allowed.astype(jnp.int32)] * HEADS_AT_ONCE, axis=0) > 0


def softmax_rows(tall, k_part, allowed):
    scores = jnp.where(allowed, nt(tall, k_part) * SCALE, -1e30)
    expo = jnp.exp(scores - jnp.max(scores, axis=-1, keepdims=True))
    return expo / jnp.sum(expo, axis=-1, keepdims=True)


def head_part(ref, step):
    steps = QUERY_HEADS // (KEY_VALUE_HEADS * HEADS_AT_ONCE)
    return ref[:, pl.ds(pl.multiple_of(step // steps * HEAD_SIZE, HEAD_SIZE), HEAD_SIZE)]


def span_of(step):
    return pl.ds(pl.multiple_of(step * SPAN, SPAN), SPAN)


def route_kernel(
    place_ref, ids_ref, gates_ref, grad_ref, select_ref, upper_ref, lower_ref, *pair_refs
):
    count = ids_ref.shape[0]
    ids, gates = ids_ref[...], gates_ref[...]
    here = lax.broadcasted_iota(jnp.int32, (count, count), 0)
    there = lax.broadcasted_iota(jnp.int32, (count, count), 1)
    group, slot = there // ROWS, there % ROWS
    present = jnp.zeros((count, count), F32)
    weight = jnp.zeros((count, count), F32)
    for i in range(EXPERTS):
        hit = ids == lax.rem(place_ref[0] + i, EXPERTS)
        found = jnp.max(hit.astype(F32), axis=-1, keepdims=True)
        amount = jnp.sum(jnp.where(hit, gates, 0.0), axis=-1, keepdims=True)
        present = jnp.where(group == i, found, present)
        weight = jnp.where(group == i, amount, weight)
    counts = nn((there < here).astype(BF16), present.astype(BF16))
    select = (present > 0.5) & (counts == slot.astype(F32))
    chosen = select.astype(F32).astype(BF16)
    select_ref[...] = chosen
    spread = jnp.where(select, weight, 0.0)
    upper = spread.astype(BF16)
    upper_ref[...] = upper
    lower_ref[...] = (spread - upper.astype(F32)).astype(BF16)
    total = EXPERTS * ROWS
    slot_weight = jnp.sum(jnp.transpose(spread), axis=-1, keepdims=True)[:total]
    picker = jnp.transpose(select.astype(F32))[:total].astype(BF16)
    line = lax.broadcasted_iota(jnp.int32, (total, 1), 0) % ROWS
    mark = jnp.where(line == ROWS - 1, place_ref[1].astype(F32), 0.0)

    def gather(step, carry):
        rows = (slot_weight * nn(picker, grad_ref[:, span_of(step)]) + mark).astype(BF16)
        for i, pair_ref in enumerate(pair_refs):
            pair_ref[:, span_of(step)] = rows[i * ROWS : (i + 1) * ROWS]
        return carry

    lax.fori_loop(0, grad_ref.shape[1] // SPAN, gather, 0)


def forward_kernel(
    lengths_ref, rank_ref, q_ref, k_ref, v_ref, gain_ref, select_ref, attn_ref, probs_ref, *row_refs
):
    count, width = q_ref.shape
    allowed = allowed_keys(lengths_ref, rank_ref, count)

    def heads(step, total):
        probs = softmax_rows(stacked(q_ref[:, span_of(step)]), head_part(k_ref, step), allowed)
        probs = probs.astype(BF16)
        probs_ref[step] = probs
        mixed = side_by_side(nn(probs, head_part(v_ref, step))).astype(BF16)
        attn_ref[:, span_of(step)] = mixed
        wide = mixed.astype(F32)
        return total + jnp.sum(wide * wide, axis=-1, keepdims=True)

    total = lax.fori_loop(0, width // SPAN, heads, jnp.zeros((count, 1), F32))
    scaling = lax.rsqrt(total / width + 1e-06)
    slots = EXPERTS * ROWS
    picker = jnp.transpose(select_ref[...].astype(F32))[:slots].astype(BF16)

    def norm(step, carry):
        wide = attn_ref[:, span_of(step)].astype(F32)
        normed = (wide * scaling * gain_ref[:, span_of(step)]).astype(BF16)
        rows = nn(picker, normed).astype(BF16)
        for i, row_ref in enumerate(row_refs):
            row_ref[:, span_of(step)] = rows[i * ROWS : (i + 1) * ROWS]
        return carry

    lax.fori_loop(0, width // SPAN, norm, 0)


def backward_kernel(
    probs_ref,
    q_ref,
    k_ref,
    v_ref,
    attn_ref,
    grad_ref,
    gain_ref,
    spread_ref,
    in0_ref,
    in1_ref,
    in2_ref,
    in3_ref,
    q_out,
    k_out,
    v_out,
    normed_grad,
):
    count, width = q_ref.shape
    in_refs = (in0_ref, in1_ref, in2_ref, in3_ref)

    def gather(step, carry):
        square, product = carry
        span = span_of(step)
        rows = jnp.concatenate([ref[:, span] for ref in in_refs], axis=0)
        grad = nn(spread_ref[:, : EXPERTS * ROWS], rows)
        normed_grad[:, span] = grad
        wide = attn_ref[:, span].astype(F32)
        square = square + jnp.sum(wide * wide, axis=-1, keepdims=True)
        product = product + jnp.sum(wide * gain_ref[:, span] * grad, axis=-1, keepdims=True)
        return square, product

    zero = jnp.zeros((count, 1), F32)
    square, product = lax.fori_loop(0, width // SPAN, gather, (zero, zero))
    scaling = lax.rsqrt(square / width + 1e-06)
    lost = scaling * scaling * scaling * (product / width)
    k_sums = [jnp.zeros((count, HEAD_SIZE), F32)] * KEY_VALUE_HEADS
    v_sums = [jnp.zeros((count, HEAD_SIZE), F32)] * KEY_VALUE_HEADS
    steps = width // SPAN // KEY_VALUE_HEADS

    for head in range(KEY_VALUE_HEADS):
        part = slice(head * HEAD_SIZE, (head + 1) * HEAD_SIZE)

        def heads(turn, sums, head=head, part=part):
            step = turn + head * steps
            span = span_of(step)
            k_part, v_part = k_ref[:, part], v_ref[:, part]
            wide = attn_ref[:, span].astype(F32)
            attn_grad = (
                grad_ref[:, span].astype(F32)
                + scaling * gain_ref[:, span] * normed_grad[:, span]
                - wide * lost
            ).astype(BF16)
            tall_q, tall_d = stacked(q_ref[:, span]), stacked(attn_grad)
            probs = probs_ref[step]
            inner = stacked(attn_grad.astype(F32) * wide)
            inner = jnp.sum(inner, axis=-1, keepdims=True)
            score_grad = probs.astype(F32) * (nt(tall_d, v_part) - inner) * SCALE
            score_grad = score_grad.astype(BF16)
            q_out[:, span] = side_by_side(nn(score_grad, k_part)).astype(BF16)
            return sums[0] + tn(score_grad, tall_q), sums[1] + tn(probs, tall_d)

        zeros = jnp.zeros((count, HEAD_SIZE), F32)
        k_sum, v_sum = lax.fori_loop(0, steps, heads, (zeros, zeros))
        k_out[:, part] = k_sum.astype(BF16)
        v_out[:, part] = v_sum.astype(BF16)


def cost(micros):
    return pl.CostEstimate(
        flops=int(micros * 1.15e9), bytes_accessed=int(micros * 3.6e6), transcendentals=0
    )


def whole():
    return pl.BlockSpec(memory_space=pltpu.VMEM)


def scalars():
    return pl.BlockSpec(memory_space=pltpu.SMEM)


def shape(*dims, dtype=BF16):
    return jax.ShapeDtypeStruct(dims, dtype)


def route(place, ids, gates, grad):
    count, width = grad.shape
    out = pl.pallas_call(
        route_kernel,
        out_shape=[shape(count, count)] * 3 + [shape(ROWS, width)] * EXPERTS,
        in_specs=[scalars()] + [whole()] * 3,
        out_specs=[whole()] * (3 + EXPERTS),
        compiler_params=pltpu.CompilerParams(vmem_limit_bytes=16 * MIB),
        cost_estimate=cost(2.5),
        name="route",
    )(place, ids, gates, grad)
    return *out[:3], list(out[3:])


def attend(lengths, rank, queries, key_rows, value_matrix, gain, select):
    count, width = queries.shape
    out = pl.pallas_call(
        forward_kernel,
        out_shape=[
            shape(count, width),
            shape(QUERY_HEADS // HEADS_AT_ONCE, HEADS_AT_ONCE * count, count),
            *([shape(ROWS, width)] * EXPERTS),
        ],
        in_specs=[scalars()] * 2 + [whole()] * 5,
        out_specs=[whole()] * (2 + EXPERTS),
        compiler_params=pltpu.CompilerParams(vmem_limit_bytes=24 * MIB),
        cost_estimate=cost(4.6),
        name="attend",
    )(lengths, rank, queries, key_rows, value_matrix, gain, select)
    return out[0], out[1], list(out[2:])


def attend_back(probs, queries, key_rows, value_matrix, attn, grad, gain, spread, in_rows):
    count, width = queries.shape
    return pl.pallas_call(
        backward_kernel,
        out_shape=[shape(count, width), shape(*key_rows.shape), shape(*key_rows.shape)],
        in_specs=[whole()] * (8 + EXPERTS),
        out_specs=[whole()] * 3,
        scratch_shapes=[pltpu.VMEM((count, width), F32)],
        compiler_params=pltpu.CompilerParams(vmem_limit_bytes=32 * MIB),
        cost_estimate=cost(5),
        name="attend_back",
    )(probs, queries, key_rows, value_matrix, attn, grad, gain, spread, *in_rows)


CHUNK = 2048


def dense_kernel(*refs):
    *in_refs, out_ref = refs
    out_ref[...] = jnp.concatenate([ref[:CAP].astype(F32) for ref in in_refs], axis=0).astype(BF16)


def by_columns(kernel, name, inputs, outs, chunk=CHUNK):
    width = inputs[0].shape[1]
    return pl.pallas_call(
        kernel,
        grid=(width // chunk,),
        in_specs=[pl.BlockSpec((v.shape[0], chunk), lambda i: (0, i)) for v in inputs],
        out_specs=[pl.BlockSpec((rows, chunk), lambda i: (0, i)) for rows in outs],
        out_shape=[shape(rows, width) for rows in outs],
        compiler_params=pltpu.CompilerParams(vmem_limit_bytes=16 * MIB),
        cost_estimate=pl.CostEstimate(
            flops=0,
            bytes_accessed=2 * width * (sum(outs) + sum(v.shape[0] for v in inputs)),
            transcendentals=0,
        ),
        name=name,
    )(*inputs)


def dense_rows(blocks):
    return by_columns(dense_kernel, "dense_rows", blocks, [CAP * EXPERTS])[0]


def add_kernel(own_ref, far_ref, *out_refs):
    total = own_ref[...].astype(F32) + far_ref[...].astype(F32)
    start = 0
    for out_ref in out_refs:
        out_ref[...] = total[start : start + out_ref.shape[0]].astype(BF16)
        start += out_ref.shape[0]


def relay_kernel(left_ref, right_ref, top_ref, low_ref, left_out, right_out):
    left, right = left_ref[...].astype(F32), right_ref[...].astype(F32)
    top = top_ref.shape[0]
    left_out[...] = jnp.concatenate(
        [left[:top] + top_ref[...].astype(F32), left[top:]], axis=0
    ).astype(BF16)
    right_out[...] = jnp.concatenate(
        [right[:top], right[top:] + low_ref[...].astype(F32)], axis=0
    ).astype(BF16)


def sum_kernel(*refs):
    in_refs, out_refs = refs[:-EXPERTS], refs[-EXPERTS:]
    total = in_refs[0][...].astype(F32)
    for ref in in_refs[1:]:
        total = total + ref[...].astype(F32)
    for i, out_ref in enumerate(out_refs):
        block = total[i * CAP : (i + 1) * CAP]
        empty = jnp.zeros((ROWS - CAP, block.shape[1]), F32)
        out_ref[...] = jnp.concatenate([block, empty], axis=0).astype(BF16)


def match_kernel(place_ref, *refs):
    *mark_refs, out_ref = refs
    total = out_ref.shape[0]
    size = total // (2 * CAP * EXPERTS)

    def keys(dims, axis, marked):
        index = lax.broadcasted_iota(jnp.int32, dims, axis)
        block, turn = index // (CAP * EXPERTS), index // CAP % EXPERTS
        away, flip = block % size, block // size
        owner = (place_ref[0] + size - away) % size * 2 + (place_ref[1] ^ flip)
        if marked:
            mask = jnp.zeros(dims, jnp.int32)
            for i, ref in enumerate(mark_refs):
                mark = ref[ROWS - 1 :, :1].astype(F32).astype(jnp.int32)
                mask = jnp.where(turn == i, mark, mask)
            owner = owner ^ mask
        return owner * (CAP * EXPERTS) + index % (CAP * EXPERTS)

    same = keys((total, 1), 0, True) == keys((1, total), 1, False)
    out_ref[...] = same.astype(F32).astype(BF16)


def match_of(place, blocks, devices):
    total = devices * CAP * EXPERTS
    return pl.pallas_call(
        match_kernel,
        grid=(1,),
        in_specs=[
            pl.BlockSpec(memory_space=pltpu.SMEM),
            *([pl.BlockSpec((ROWS, HEAD_SIZE), lambda i: (0, 0))] * len(blocks)),
        ],
        out_specs=pl.BlockSpec((total, total), lambda i: (0, 0)),
        out_shape=shape(total, total),
        compiler_params=pltpu.CompilerParams(vmem_limit_bytes=16 * MIB),
        cost_estimate=cost(1),
        name="match",
    )(place, *blocks)


def layer_kernel(home_ref, moved_ref, upper_ref, lower_ref, *refs):
    *in_refs, out_ref = refs
    rows = jnp.concatenate([ref[...] for ref in in_refs], axis=0)
    slots = rows.shape[0]
    added = nn(upper_ref[:, :slots], rows) + nn(lower_ref[:, :slots], rows)
    out_ref[...] = (moved_ref[0].astype(F32) + added).astype(BF16)


def layer_rows(home, moved, upper, lower, rows):
    _, count, width = moved.shape
    wide = lambda n: pl.BlockSpec((n, CHUNK), lambda i, home: (0, i))
    fixed = pl.BlockSpec(upper.shape, lambda i, home: (0, 0))
    return pl.pallas_call(
        layer_kernel,
        grid_spec=pltpu.PrefetchScalarGridSpec(
            num_scalar_prefetch=1,
            grid=(width // CHUNK,),
            in_specs=[
                pl.BlockSpec((1, count, CHUNK), lambda i, home: (home[0], 0, i)),
                fixed,
                fixed,
                *([wide(ROWS)] * EXPERTS),
            ],
            out_specs=wide(count),
        ),
        out_shape=shape(count, width),
        compiler_params=pltpu.CompilerParams(vmem_limit_bytes=58 * MIB),
        cost_estimate=cost(4),
        name="layer_rows",
    )(home, moved, upper, lower, *rows)


def joined(refs):
    return jnp.concatenate([ref[...].astype(F32) for ref in refs], axis=0).astype(BF16)


def hidden_grad_kernel(*refs):
    *grad_refs, mats_ref, out_ref = refs

    @pl.when(pl.program_id(0) == 0)
    def _():
        out_ref[...] = jnp.zeros_like(out_ref)

    out_ref[...] += nt(joined(grad_refs), mats_ref[0])


def hidden_grad_of(grads, mats):
    each, width = grads[0].shape
    total, units = len(grads) * each, mats.shape[1]
    return pl.pallas_call(
        hidden_grad_kernel,
        grid=(width // CHUNK,),
        in_specs=[
            *([pl.BlockSpec((each, CHUNK), lambda i: (0, i))] * len(grads)),
            pl.BlockSpec((1, units, CHUNK), lambda i: (2, 0, i)),
        ],
        out_specs=pl.BlockSpec((total, units), lambda i: (0, 0)),
        out_shape=shape(total, units, dtype=F32),
        compiler_params=pltpu.CompilerParams(vmem_limit_bytes=58 * MIB),
        cost_estimate=cost(4),
        name="hidden_grad",
    )(*grads, mats)


def experts_in_kernel(steps, blocks, *refs):
    row_refs = refs[:blocks]
    mats_ref, match_ref, hidden_grad, far_ref, hidden_ref, own_ref = refs[blocks : blocks + 6]
    gate_in, up_in, both = refs[blocks + 6 :]
    step = pl.program_id(0)
    units = mats_ref.shape[1]

    @pl.when(step == 0)
    def _():
        gate_in[...] = jnp.zeros_like(gate_in)
        up_in[...] = jnp.zeros_like(up_in)

    @pl.when(step < steps)
    def _():
        rows = joined(row_refs)
        gate_in[...] += nt(rows, mats_ref[0])
        up_in[...] += nt(rows, mats_ref[1])

    @pl.when(step == steps - 1)
    def _():
        match = match_ref[...]
        rest = hidden_grad[...]
        grad = jnp.zeros_like(rest)
        for _ in range(3):
            piece = rest.astype(BF16)
            grad = grad + nn(match, piece)
            rest = rest - piece.astype(F32)
        gate = gate_in[...]
        up = up_in[...]
        sigma = jax.nn.sigmoid(gate)
        active = gate * sigma
        hidden_ref[...] = tn(match, (active * up).astype(BF16)).astype(BF16)
        both[:, :units] = (grad * up * sigma * (1.0 + gate * (1.0 - sigma))).astype(BF16)
        both[:, units:] = (grad * active).astype(BF16)
        own_ref[...] = both[: own_ref.shape[0]]

    @pl.when(step >= steps)
    def _():
        mats = jnp.concatenate([mats_ref[0], mats_ref[1]], axis=0)
        far_ref[...] = nn(both[far_ref.shape[0] :], mats).astype(BF16)


def experts_own_kernel(both_ref, mats_ref, own_ref):
    mats = jnp.concatenate([mats_ref[0], mats_ref[1]], axis=0)
    own_ref[...] = nn(both_ref[...], mats).astype(BF16)


def experts_own(both, mats):
    half, width = both.shape[0], mats.shape[2]
    units = mats.shape[1]
    return pl.pallas_call(
        experts_own_kernel,
        grid=(width // CHUNK,),
        in_specs=[
            pl.BlockSpec(both.shape, lambda i: (0, 0)),
            pl.BlockSpec((2, units, CHUNK), lambda i: (0, 0, i)),
        ],
        out_specs=pl.BlockSpec((half, CHUNK), lambda i: (0, i)),
        out_shape=shape(half, width),
        compiler_params=pltpu.CompilerParams(vmem_limit_bytes=58 * MIB),
        cost_estimate=cost(3),
        name="experts_own",
    )(both, mats)


def experts_in(rows, mats, match, hidden_grad):
    blocks = len(rows)
    each, width = rows[0].shape
    total = blocks * each
    units = mats.shape[1]
    steps = width // CHUNK
    half = total // 2
    first = lambda i: (0, jnp.minimum(i, steps - 1))
    last = lambda i: (0, jnp.maximum(i - steps, 0))
    fixed = lambda i: (0, 0)
    return pl.pallas_call(
        functools.partial(experts_in_kernel, steps, blocks),
        grid=(2 * steps,),
        in_specs=[
            *([pl.BlockSpec((each, CHUNK), first)] * blocks),
            pl.BlockSpec((2, units, CHUNK), lambda i: (0, 0, lax.rem(i, steps))),
            pl.BlockSpec((total, total), fixed),
            pl.BlockSpec((total, units), fixed),
        ],
        out_specs=[
            pl.BlockSpec((half, CHUNK), last),
            pl.BlockSpec((total, units), fixed),
            pl.BlockSpec((half, 2 * units), fixed),
        ],
        out_shape=[shape(half, width), shape(total, units), shape(half, 2 * units)],
        scratch_shapes=[pltpu.VMEM((total, units), F32)] * 2 + [pltpu.VMEM((total, 2 * units), BF16)],
        compiler_params=pltpu.CompilerParams(vmem_limit_bytes=58 * MIB),
        cost_estimate=cost(10),
        name="experts_in",
    )(*rows, mats, match, hidden_grad)


def experts_out_kernel(hidden_ref, mats_ref, own_ref, far_ref):
    half = own_ref.shape[0]
    far_ref[...] = nn(hidden_ref[half:], mats_ref[0]).astype(BF16)
    own_ref[...] = nn(hidden_ref[:half], mats_ref[0]).astype(BF16)


def experts_out(hidden, mats):
    total, units = hidden.shape
    width = mats.shape[2]
    half = total // 2
    return pl.pallas_call(
        experts_out_kernel,
        grid=(width // CHUNK,),
        in_specs=[
            pl.BlockSpec((total, units), lambda i: (0, 0)),
            pl.BlockSpec((1, units, CHUNK), lambda i: (2, 0, i)),
        ],
        out_specs=[pl.BlockSpec((half, CHUNK), lambda i: (0, i))] * 2,
        out_shape=[shape(half, width)] * 2,
        compiler_params=pltpu.CompilerParams(vmem_limit_bytes=58 * MIB),
        cost_estimate=cost(2),
        name="experts_out",
    )(hidden, mats)


def shifted(value, axis, step):
    size = lax.axis_size(axis)
    if step % size == 0:
        return value
    return lax.ppermute(value, axis, [(i, (i + step) % size) for i in range(size)])


def swapped(value):
    return lax.ppermute(value, "c", [(0, 1), (1, 0)])


def to_experts(blocks):
    return [shifted(blocks[s], "y", s) for s in range(EXPERTS)]


def from_experts(blocks):
    return [shifted(blocks[s], "y", -s) for s in range(EXPERTS)]


def along_x(block):
    return [shifted(block, "x", s) for s in range(lax.axis_size("x"))]


def both_cores(blocks):
    return blocks + [swapped(b) for b in blocks]


TOP = 32


def add_far(own, far):
    each = own.shape[0] // lax.axis_size("x")
    sizes = [each, each, TOP, each - TOP, each]
    return by_columns(add_kernel, "add_rows", [own, swapped(far)], sizes)


def half_way(blocks):
    mine, left, top, low, right = blocks
    parts = [left, right, shifted(top, "x", -1), shifted(low, "x", 1)]
    left, right = by_columns(relay_kernel, "relay_rows", parts, [left.shape[0]] * 2)
    return [mine, shifted(left, "x", -1), shifted(right, "x", 1)]


def total_of(parts):
    return by_columns(sum_kernel, "sum_rows", parts, [ROWS] * EXPERTS)


def by_mask(mask, *values):
    ranks = lax.axis_size("x") * lax.axis_size("c")

    def branch(k):
        pairs = [(i, i ^ k) for i in range(ranks)]
        return lambda *v: tuple(lax.ppermute(one, ("x", "c"), pairs) for one in v)

    return lax.switch(mask - 1, [branch(k) for k in range(1, ranks)], *values)


def after(values, other):
    return lax.optimization_barrier((values, other))[0]


def shards(
    queries,
    key_rows,
    value_matrix,
    doc_lengths,
    seq_plan,
    norm_gain,
    w_gate,
    w_up,
    w_down,
    expert_ids,
    gate_weights,
    out_grad,
):
    queries, key_rows, value_matrix, out_grad = queries[0], key_rows[0], value_matrix[0], out_grad[0]
    w_gate, w_up, w_down = w_gate[0], w_up[0], w_down[0]
    route_ids, route_gates = expert_ids[0], gate_weights[0]
    x, c, y = lax.axis_index("x"), lax.axis_index("c"), lax.axis_index("y")
    x_size = lax.axis_size("x")
    ranks = 2 * x_size
    rank = x * 2 + c
    count, width = queries.shape
    mask = seq_plan[0, 0]
    gain = norm_gain[None]
    lengths = doc_lengths[0]
    rank_word = jnp.full((1,), rank, jnp.int32)

    units = w_gate.shape[1] // ranks
    pieces = jnp.stack(
        [
            lax.dynamic_slice_in_dim(m, rank * units, units, 0)
            for m in (jnp.transpose(w_gate), jnp.transpose(w_up), w_down)
        ]
    )
    mats = lax.all_gather(pieces, "z", axis=1, tiled=True)

    place = jnp.stack([y, mask]).astype(jnp.int32)
    select, upper, lower, pair_blocks = route(
        *after((place, route_ids, route_gates, out_grad), pieces)
    )
    pair_blocks = to_experts(pair_blocks)
    (select_home,) = by_mask(mask, select)
    pair_block = dense_rows(pair_blocks)
    match = match_of(jnp.stack([x, c]).astype(jnp.int32), pair_blocks, 2 * x_size)
    queries, select_home = after((queries, select_home), (pair_block, match))
    attn, probs, row_blocks = attend(
        lengths, rank_word, queries, key_rows, value_matrix, gain, select_home
    )
    pairs_x = along_x(pair_block)
    row_block = dense_rows(to_experts(row_blocks))
    (grad_home,) = by_mask(mask, after(out_grad, (pairs_x, row_block)))
    row_block, attn_home = after((row_block, attn), grad_home)
    moved = lax.all_gather(attn_home, ("x", "c"))
    hidden_grad = hidden_grad_of(both_cores(pairs_x), mats)
    rows_x, hidden_grad = lax.optimization_barrier((along_x(row_block), hidden_grad))
    rows = both_cores(rows_x)

    far_in, hidden, both = experts_in(rows, mats, match, hidden_grad)
    own_in = experts_own(both, mats)
    in_blocks = add_far(own_in, far_in)
    hidden = after(hidden, in_blocks)
    own_out, far_out = experts_out(hidden, mats)
    out_blocks = add_far(*after((own_out, far_out), in_blocks))
    in_parts = half_way(in_blocks)
    out_parts = half_way(out_blocks)
    in_sums = total_of(in_parts)
    in_rows = from_experts(in_sums)
    out_sums = total_of([after(out_parts[0], in_sums[0]), *out_parts[1:]])
    out_rows = from_experts(out_sums)
    in_rows = after(in_rows, out_sums)

    q_home, k_home, v_home = attend_back(
        probs, queries, key_rows, value_matrix, attn, grad_home, gain, select_home, in_rows
    )
    layer = layer_rows(rank_word ^ mask, moved, after(upper, k_home), lower, out_rows)
    return (layer[None], q_home[None], k_home[None], v_home[None])


def solution(mesh):
    fine = Mesh(mesh.devices.reshape(4, 2, 4, 8), ("x", "c", "y", "z"))
    every = ("x", "c", "y", "z")
    expert = ("y", "z")
    return jax.shard_map(
        shards,
        mesh=fine,
        in_specs=(
            P(every),
            P(every),
            P(every),
            P(expert),
            P(expert),
            P(),
            P(expert),
            P(expert),
            P(expert),
            P(every),
            P(every),
            P(every),
        ),
        out_specs=(P(every), P(every), P(every), P(every)),
        check_vma=False,
    )
```

```python
import functools

import jax
import jax.numpy as jnp
from jax import lax
from jax.experimental import pallas as pl
from jax.experimental.pallas import tpu as pltpu
from jax.sharding import Mesh
from jax.sharding import PartitionSpec as P

HEAD_SIZE = 128
QUERY_HEADS = 32
KEY_VALUE_HEADS = 2
CAP = 14
ROWS = 16
EXPERTS = 4
HEADS_AT_ONCE = 16
SPAN = HEADS_AT_ONCE * HEAD_SIZE
SCALE = HEAD_SIZE ** (-0.5)
F32 = jnp.float32
BF16 = jnp.bfloat16
MIB = 1 << 20


def nt(left, right):
    return lax.dot_general(left, right, (((1,), (1,)), ((), ())), preferred_element_type=F32)


def tn(left, right):
    return lax.dot_general(left, right, (((0,), (0,)), ((), ())), preferred_element_type=F32)


def nn(left, right):
    return jnp.dot(left, right, preferred_element_type=F32)


def stacked(wide):
    return jnp.concatenate(
        [wide[:, i * HEAD_SIZE : (i + 1) * HEAD_SIZE] for i in range(HEADS_AT_ONCE)], axis=0
    )


def side_by_side(tall):
    count = tall.shape[0] // HEADS_AT_ONCE
    return jnp.concatenate(
        [tall[i * count : (i + 1) * count] for i in range(HEADS_AT_ONCE)], axis=1
    )


def allowed_keys(lengths_ref, rank_ref, count):
    rank = rank_ref[0]
    here = lax.broadcasted_iota(jnp.int32, (count, count), 0)
    there = lax.broadcasted_iota(jnp.int32, (count, count), 1)
    bound = jnp.int32(0)
    mine = jnp.zeros((count, count), jnp.int32)
    other = jnp.zeros((count, count), jnp.int32)
    for i in range(lengths_ref.shape[1]):
        bound = bound + lengths_ref[rank, i]
        mine = mine + (here >= bound).astype(jnp.int32)
        other = other + (there >= bound).astype(jnp.int32)
    allowed = (mine == other) & (there <= here)
    return jnp.concatenate([allowed.astype(jnp.int32)] * HEADS_AT_ONCE, axis=0) > 0


def softmax_rows(tall, k_part, allowed):
    scores = jnp.where(allowed, nt(tall, k_part) * SCALE, -1e30)
    expo = jnp.exp(scores - jnp.max(scores, axis=-1, keepdims=True))
    return expo / jnp.sum(expo, axis=-1, keepdims=True)


def head_part(ref, step):
    steps = QUERY_HEADS // (KEY_VALUE_HEADS * HEADS_AT_ONCE)
    return ref[:, pl.ds(pl.multiple_of(step // steps * HEAD_SIZE, HEAD_SIZE), HEAD_SIZE)]


def span_of(step):
    return pl.ds(pl.multiple_of(step * SPAN, SPAN), SPAN)


def route_kernel(
    place_ref, ids_ref, gates_ref, grad_ref, select_ref, upper_ref, lower_ref, *pair_refs
):
    count = ids_ref.shape[0]
    ids, gates = ids_ref[...], gates_ref[...]
    here = lax.broadcasted_iota(jnp.int32, (count, count), 0)
    there = lax.broadcasted_iota(jnp.int32, (count, count), 1)
    group, slot = there // ROWS, there % ROWS
    present = jnp.zeros((count, count), F32)
    weight = jnp.zeros((count, count), F32)
    for i in range(EXPERTS):
        hit = ids == lax.rem(place_ref[0] + i, EXPERTS)
        found = jnp.max(hit.astype(F32), axis=-1, keepdims=True)
        amount = jnp.sum(jnp.where(hit, gates, 0.0), axis=-1, keepdims=True)
        present = jnp.where(group == i, found, present)
        weight = jnp.where(group == i, amount, weight)
    counts = nn((there < here).astype(BF16), present.astype(BF16))
    select = (present > 0.5) & (counts == slot.astype(F32))
    chosen = select.astype(F32).astype(BF16)
    select_ref[...] = chosen
    spread = jnp.where(select, weight, 0.0)
    upper = spread.astype(BF16)
    upper_ref[...] = upper
    lower_ref[...] = (spread - upper.astype(F32)).astype(BF16)
    total = EXPERTS * ROWS
    slot_weight = jnp.sum(jnp.transpose(spread), axis=-1, keepdims=True)[:total]
    picker = jnp.transpose(select.astype(F32))[:total].astype(BF16)
    line = lax.broadcasted_iota(jnp.int32, (total, 1), 0) % ROWS
    mark = jnp.where(line == ROWS - 1, place_ref[1].astype(F32), 0.0)

    def gather(step, carry):
        rows = (slot_weight * nn(picker, grad_ref[:, span_of(step)]) + mark).astype(BF16)
        for i, pair_ref in enumerate(pair_refs):
            pair_ref[:, span_of(step)] = rows[i * ROWS : (i + 1) * ROWS]
        return carry

    lax.fori_loop(0, grad_ref.shape[1] // SPAN, gather, 0)


def forward_kernel(
    lengths_ref, rank_ref, q_ref, k_ref, v_ref, gain_ref, select_ref, attn_ref, probs_ref, *row_refs
):
    count, width = q_ref.shape
    allowed = allowed_keys(lengths_ref, rank_ref, count)

    def heads(step, total):
        probs = softmax_rows(stacked(q_ref[:, span_of(step)]), head_part(k_ref, step), allowed)
        probs = probs.astype(BF16)
        probs_ref[step] = probs
        mixed = side_by_side(nn(probs, head_part(v_ref, step))).astype(BF16)
        attn_ref[:, span_of(step)] = mixed
        wide = mixed.astype(F32)
        return total + jnp.sum(wide * wide, axis=-1, keepdims=True)

    total = lax.fori_loop(0, width // SPAN, heads, jnp.zeros((count, 1), F32))
    scaling = lax.rsqrt(total / width + 1e-06)
    slots = EXPERTS * ROWS
    picker = jnp.transpose(select_ref[...].astype(F32))[:slots].astype(BF16)

    def norm(step, carry):
        wide = attn_ref[:, span_of(step)].astype(F32)
        normed = (wide * scaling * gain_ref[:, span_of(step)]).astype(BF16)
        rows = nn(picker, normed).astype(BF16)
        for i, row_ref in enumerate(row_refs):
            row_ref[:, span_of(step)] = rows[i * ROWS : (i + 1) * ROWS]
        return carry

    lax.fori_loop(0, width // SPAN, norm, 0)


def backward_kernel(
    probs_ref,
    q_ref,
    k_ref,
    v_ref,
    attn_ref,
    grad_ref,
    gain_ref,
    spread_ref,
    in0_ref,
    in1_ref,
    in2_ref,
    in3_ref,
    q_out,
    k_out,
    v_out,
    normed_grad,
):
    count, width = q_ref.shape
    in_refs = (in0_ref, in1_ref, in2_ref, in3_ref)

    def gather(step, carry):
        square, product = carry
        span = span_of(step)
        rows = jnp.concatenate([ref[:, span] for ref in in_refs], axis=0)
        grad = nn(spread_ref[:, : EXPERTS * ROWS], rows)
        normed_grad[:, span] = grad
        wide = attn_ref[:, span].astype(F32)
        square = square + jnp.sum(wide * wide, axis=-1, keepdims=True)
        product = product + jnp.sum(wide * gain_ref[:, span] * grad, axis=-1, keepdims=True)
        return square, product

    zero = jnp.zeros((count, 1), F32)
    square, product = lax.fori_loop(0, width // SPAN, gather, (zero, zero))
    scaling = lax.rsqrt(square / width + 1e-06)
    lost = scaling * scaling * scaling * (product / width)
    k_sums = [jnp.zeros((count, HEAD_SIZE), F32)] * KEY_VALUE_HEADS
    v_sums = [jnp.zeros((count, HEAD_SIZE), F32)] * KEY_VALUE_HEADS
    steps = width // SPAN // KEY_VALUE_HEADS

    for head in range(KEY_VALUE_HEADS):
        part = slice(head * HEAD_SIZE, (head + 1) * HEAD_SIZE)

        def heads(turn, sums, head=head, part=part):
            step = turn + head * steps
            span = span_of(step)
            k_part, v_part = k_ref[:, part], v_ref[:, part]
            wide = attn_ref[:, span].astype(F32)
            attn_grad = (
                grad_ref[:, span].astype(F32)
                + scaling * gain_ref[:, span] * normed_grad[:, span]
                - wide * lost
            ).astype(BF16)
            tall_q, tall_d = stacked(q_ref[:, span]), stacked(attn_grad)
            probs = probs_ref[step]
            inner = stacked(attn_grad.astype(F32) * wide)
            inner = jnp.sum(inner, axis=-1, keepdims=True)
            score_grad = probs.astype(F32) * (nt(tall_d, v_part) - inner) * SCALE
            score_grad = score_grad.astype(BF16)
            q_out[:, span] = side_by_side(nn(score_grad, k_part)).astype(BF16)
            return sums[0] + tn(score_grad, tall_q), sums[1] + tn(probs, tall_d)

        zeros = jnp.zeros((count, HEAD_SIZE), F32)
        k_sum, v_sum = lax.fori_loop(0, steps, heads, (zeros, zeros))
        k_out[:, part] = k_sum.astype(BF16)
        v_out[:, part] = v_sum.astype(BF16)


def cost(micros):
    return pl.CostEstimate(
        flops=int(micros * 1.15e9), bytes_accessed=int(micros * 3.6e6), transcendentals=0
    )


def whole():
    return pl.BlockSpec(memory_space=pltpu.VMEM)


def scalars():
    return pl.BlockSpec(memory_space=pltpu.SMEM)


def shape(*dims, dtype=BF16):
    return jax.ShapeDtypeStruct(dims, dtype)


def route(place, ids, gates, grad):
    count, width = grad.shape
    out = pl.pallas_call(
        route_kernel,
        out_shape=[shape(count, count)] * 3 + [shape(ROWS, width)] * EXPERTS,
        in_specs=[scalars()] + [whole()] * 3,
        out_specs=[whole()] * (3 + EXPERTS),
        compiler_params=pltpu.CompilerParams(vmem_limit_bytes=16 * MIB),
        cost_estimate=cost(2.5),
        name="route",
    )(place, ids, gates, grad)
    return *out[:3], list(out[3:])


def attend(lengths, rank, queries, key_rows, value_matrix, gain, select):
    count, width = queries.shape
    out = pl.pallas_call(
        forward_kernel,
        out_shape=[
            shape(count, width),
            shape(QUERY_HEADS // HEADS_AT_ONCE, HEADS_AT_ONCE * count, count),
            *([shape(ROWS, width)] * EXPERTS),
        ],
        in_specs=[scalars()] * 2 + [whole()] * 5,
        out_specs=[whole()] * (2 + EXPERTS),
        compiler_params=pltpu.CompilerParams(vmem_limit_bytes=24 * MIB),
        cost_estimate=cost(4.6),
        name="attend",
    )(lengths, rank, queries, key_rows, value_matrix, gain, select)
    return out[0], out[1], list(out[2:])


def attend_back(probs, queries, key_rows, value_matrix, attn, grad, gain, spread, in_rows):
    count, width = queries.shape
    return pl.pallas_call(
        backward_kernel,
        out_shape=[shape(count, width), shape(*key_rows.shape), shape(*key_rows.shape)],
        in_specs=[whole()] * (8 + EXPERTS),
        out_specs=[whole()] * 3,
        scratch_shapes=[pltpu.VMEM((count, width), F32)],
        compiler_params=pltpu.CompilerParams(vmem_limit_bytes=32 * MIB),
        cost_estimate=cost(5),
        name="attend_back",
    )(probs, queries, key_rows, value_matrix, attn, grad, gain, spread, *in_rows)


CHUNK = 2048


def dense_kernel(*refs):
    *in_refs, out_ref = refs
    out_ref[...] = jnp.concatenate([ref[:CAP].astype(F32) for ref in in_refs], axis=0).astype(BF16)


def by_columns(kernel, name, inputs, outs, chunk=CHUNK):
    width = inputs[0].shape[1]
    return pl.pallas_call(
        kernel,
        grid=(width // chunk,),
        in_specs=[pl.BlockSpec((v.shape[0], chunk), lambda i: (0, i)) for v in inputs],
        out_specs=[pl.BlockSpec((rows, chunk), lambda i: (0, i)) for rows in outs],
        out_shape=[shape(rows, width) for rows in outs],
        compiler_params=pltpu.CompilerParams(vmem_limit_bytes=16 * MIB),
        cost_estimate=pl.CostEstimate(
            flops=0,
            bytes_accessed=2 * width * (sum(outs) + sum(v.shape[0] for v in inputs)),
            transcendentals=0,
        ),
        name=name,
    )(*inputs)


def dense_rows(blocks):
    return by_columns(dense_kernel, "dense_rows", blocks, [CAP * EXPERTS])[0]


def add_kernel(own_ref, far_ref, *out_refs):
    total = own_ref[...].astype(F32) + far_ref[...].astype(F32)
    start = 0
    for out_ref in out_refs:
        out_ref[...] = total[start : start + out_ref.shape[0]].astype(BF16)
        start += out_ref.shape[0]


def relay_kernel(left_ref, right_ref, top_ref, low_ref, left_out, right_out):
    left, right = left_ref[...].astype(F32), right_ref[...].astype(F32)
    top = top_ref.shape[0]
    left_out[...] = jnp.concatenate(
        [left[:top] + top_ref[...].astype(F32), left[top:]], axis=0
    ).astype(BF16)
    right_out[...] = jnp.concatenate(
        [right[:top], right[top:] + low_ref[...].astype(F32)], axis=0
    ).astype(BF16)


def sum_kernel(*refs):
    in_refs, out_refs = refs[:-EXPERTS], refs[-EXPERTS:]
    total = in_refs[0][...].astype(F32)
    for ref in in_refs[1:]:
        total = total + ref[...].astype(F32)
    for i, out_ref in enumerate(out_refs):
        block = total[i * CAP : (i + 1) * CAP]
        empty = jnp.zeros((ROWS - CAP, block.shape[1]), F32)
        out_ref[...] = jnp.concatenate([block, empty], axis=0).astype(BF16)


def match_kernel(place_ref, *refs):
    *mark_refs, out_ref = refs
    total = out_ref.shape[0]
    size = total // (2 * CAP * EXPERTS)

    def keys(dims, axis, marked):
        index = lax.broadcasted_iota(jnp.int32, dims, axis)
        block, turn = index // (CAP * EXPERTS), index // CAP % EXPERTS
        away, flip = block % size, block // size
        owner = (place_ref[0] + size - away) % size * 2 + (place_ref[1] ^ flip)
        if marked:
            mask = jnp.zeros(dims, jnp.int32)
            for i, ref in enumerate(mark_refs):
                mark = ref[ROWS - 1 :, :1].astype(F32).astype(jnp.int32)
                mask = jnp.where(turn == i, mark, mask)
            owner = owner ^ mask
        return owner * (CAP * EXPERTS) + index % (CAP * EXPERTS)

    same = keys((total, 1), 0, True) == keys((1, total), 1, False)
    out_ref[...] = same.astype(F32).astype(BF16)


def match_of(place, blocks, devices):
    total = devices * CAP * EXPERTS
    return pl.pallas_call(
        match_kernel,
        grid=(1,),
        in_specs=[
            pl.BlockSpec(memory_space=pltpu.SMEM),
            *([pl.BlockSpec((ROWS, HEAD_SIZE), lambda i: (0, 0))] * len(blocks)),
        ],
        out_specs=pl.BlockSpec((total, total), lambda i: (0, 0)),
        out_shape=shape(total, total),
        compiler_params=pltpu.CompilerParams(vmem_limit_bytes=16 * MIB),
        cost_estimate=cost(1),
        name="match",
    )(place, *blocks)


def layer_kernel(home_ref, moved_ref, upper_ref, lower_ref, *refs):
    *in_refs, out_ref = refs
    rows = jnp.concatenate([ref[...] for ref in in_refs], axis=0)
    slots = rows.shape[0]
    added = nn(upper_ref[:, :slots], rows) + nn(lower_ref[:, :slots], rows)
    out_ref[...] = (moved_ref[0].astype(F32) + added).astype(BF16)


def layer_rows(home, moved, upper, lower, rows):
    _, count, width = moved.shape
    wide = lambda n: pl.BlockSpec((n, CHUNK), lambda i, home: (0, i))
    fixed = pl.BlockSpec(upper.shape, lambda i, home: (0, 0))
    return pl.pallas_call(
        layer_kernel,
        grid_spec=pltpu.PrefetchScalarGridSpec(
            num_scalar_prefetch=1,
            grid=(width // CHUNK,),
            in_specs=[
                pl.BlockSpec((1, count, CHUNK), lambda i, home: (home[0], 0, i)),
                fixed,
                fixed,
                *([wide(ROWS)] * EXPERTS),
            ],
            out_specs=wide(count),
        ),
        out_shape=shape(count, width),
        compiler_params=pltpu.CompilerParams(vmem_limit_bytes=58 * MIB),
        cost_estimate=cost(4),
        name="layer_rows",
    )(home, moved, upper, lower, *rows)


def joined(refs):
    return jnp.concatenate([ref[...].astype(F32) for ref in refs], axis=0).astype(BF16)


def hidden_grad_kernel(*refs):
    *grad_refs, mats_ref, out_ref = refs

    @pl.when(pl.program_id(0) == 0)
    def _():
        out_ref[...] = jnp.zeros_like(out_ref)

    out_ref[...] += nt(joined(grad_refs), mats_ref[0])


def hidden_grad_of(grads, mats):
    each, width = grads[0].shape
    total, units = len(grads) * each, mats.shape[1]
    return pl.pallas_call(
        hidden_grad_kernel,
        grid=(width // CHUNK,),
        in_specs=[
            *([pl.BlockSpec((each, CHUNK), lambda i: (0, i))] * len(grads)),
            pl.BlockSpec((1, units, CHUNK), lambda i: (2, 0, i)),
        ],
        out_specs=pl.BlockSpec((total, units), lambda i: (0, 0)),
        out_shape=shape(total, units, dtype=F32),
        compiler_params=pltpu.CompilerParams(vmem_limit_bytes=58 * MIB),
        cost_estimate=cost(4),
        name="hidden_grad",
    )(*grads, mats)


def experts_in_kernel(steps, blocks, *refs):
    row_refs = refs[:blocks]
    mats_ref, match_ref, hidden_grad, far_ref, hidden_ref, own_ref = refs[blocks : blocks + 6]
    gate_in, up_in, both = refs[blocks + 6 :]
    step = pl.program_id(0)
    units = mats_ref.shape[1]

    @pl.when(step == 0)
    def _():
        gate_in[...] = jnp.zeros_like(gate_in)
        up_in[...] = jnp.zeros_like(up_in)

    @pl.when(step < steps)
    def _():
        rows = joined(row_refs)
        gate_in[...] += nt(rows, mats_ref[0])
        up_in[...] += nt(rows, mats_ref[1])

    @pl.when(step == steps - 1)
    def _():
        match = match_ref[...]
        rest = hidden_grad[...]
        grad = jnp.zeros_like(rest)
        for _ in range(3):
            piece = rest.astype(BF16)
            grad = grad + nn(match, piece)
            rest = rest - piece.astype(F32)
        gate = gate_in[...]
        up = up_in[...]
        sigma = jax.nn.sigmoid(gate)
        active = gate * sigma
        hidden_ref[...] = tn(match, (active * up).astype(BF16)).astype(BF16)
        both[:, :units] = (grad * up * sigma * (1.0 + gate * (1.0 - sigma))).astype(BF16)
        both[:, units:] = (grad * active).astype(BF16)
        own_ref[...] = both[: own_ref.shape[0]]

    @pl.when(step >= steps)
    def _():
        mats = jnp.concatenate([mats_ref[0], mats_ref[1]], axis=0)
        far_ref[...] = nn(both[far_ref.shape[0] :], mats).astype(BF16)


def experts_in(rows, mats, match, hidden_grad):
    blocks = len(rows)
    each, width = rows[0].shape
    total = blocks * each
    units = mats.shape[1]
    steps = width // CHUNK
    half = total // 2
    first = lambda i: (0, jnp.minimum(i, steps - 1))
    last = lambda i: (0, jnp.maximum(i - steps, 0))
    fixed = lambda i: (0, 0)
    return pl.pallas_call(
        functools.partial(experts_in_kernel, steps, blocks),
        grid=(2 * steps,),
        in_specs=[
            *([pl.BlockSpec((each, CHUNK), first)] * blocks),
            pl.BlockSpec((2, units, CHUNK), lambda i: (0, 0, lax.rem(i, steps))),
            pl.BlockSpec((total, total), fixed),
            pl.BlockSpec((total, units), fixed),
        ],
        out_specs=[
            pl.BlockSpec((half, CHUNK), last),
            pl.BlockSpec((total, units), fixed),
            pl.BlockSpec((half, 2 * units), fixed),
        ],
        out_shape=[shape(half, width), shape(total, units), shape(half, 2 * units)],
        scratch_shapes=[pltpu.VMEM((total, units), F32)] * 2 + [pltpu.VMEM((total, 2 * units), BF16)],
        compiler_params=pltpu.CompilerParams(vmem_limit_bytes=58 * MIB),
        cost_estimate=cost(10),
        name="experts_in",
    )(*rows, mats, match, hidden_grad)


def experts_out_kernel(both_ref, hidden_ref, mats_ref, own_in, own_out, far_out):
    half = own_out.shape[0]
    gates = jnp.concatenate([mats_ref[0], mats_ref[1]], axis=0)
    own_in[...] = nn(both_ref[...], gates).astype(BF16)
    far_out[...] = nn(hidden_ref[half:], mats_ref[2]).astype(BF16)
    own_out[...] = nn(hidden_ref[:half], mats_ref[2]).astype(BF16)


def experts_out(both, hidden, mats):
    half, units = both.shape[0], mats.shape[1]
    width = mats.shape[2]
    return pl.pallas_call(
        experts_out_kernel,
        grid=(width // CHUNK,),
        in_specs=[
            pl.BlockSpec(both.shape, lambda i: (0, 0)),
            pl.BlockSpec(hidden.shape, lambda i: (0, 0)),
            pl.BlockSpec((3, units, CHUNK), lambda i: (0, 0, i)),
        ],
        out_specs=[pl.BlockSpec((half, CHUNK), lambda i: (0, i))] * 3,
        out_shape=[shape(half, width)] * 3,
        compiler_params=pltpu.CompilerParams(vmem_limit_bytes=58 * MIB),
        cost_estimate=cost(5),
        name="experts_out",
    )(both, hidden, mats)


def shifted(value, axis, step):
    size = lax.axis_size(axis)
    if step % size == 0:
        return value
    return lax.ppermute(value, axis, [(i, (i + step) % size) for i in range(size)])


def swapped(value):
    return lax.ppermute(value, "c", [(0, 1), (1, 0)])


def to_experts(blocks):
    return [shifted(blocks[s], "y", s) for s in range(EXPERTS)]


def from_experts(blocks):
    return [shifted(blocks[s], "y", -s) for s in range(EXPERTS)]


def along_x(block):
    return [shifted(block, "x", s) for s in range(lax.axis_size("x"))]


def both_cores(blocks):
    return blocks + [swapped(b) for b in blocks]


TOP = 32


def add_far(own, far):
    each = own.shape[0] // lax.axis_size("x")
    sizes = [each, each, TOP, each - TOP, each]
    return by_columns(add_kernel, "add_rows", [own, swapped(far)], sizes)


def half_way(blocks):
    mine, left, top, low, right = blocks
    parts = [left, right, shifted(top, "x", -1), shifted(low, "x", 1)]
    left, right = by_columns(relay_kernel, "relay_rows", parts, [left.shape[0]] * 2)
    return [mine, shifted(left, "x", -1), shifted(right, "x", 1)]


def total_of(parts):
    return by_columns(sum_kernel, "sum_rows", parts, [ROWS] * EXPERTS)


def by_mask(mask, *values):
    ranks = lax.axis_size("x") * lax.axis_size("c")

    def branch(k):
        pairs = [(i, i ^ k) for i in range(ranks)]
        return lambda *v: tuple(lax.ppermute(one, ("x", "c"), pairs) for one in v)

    return lax.switch(mask - 1, [branch(k) for k in range(1, ranks)], *values)


def after(values, other):
    return lax.optimization_barrier((values, other))[0]


def shards(
    queries,
    key_rows,
    value_matrix,
    doc_lengths,
    seq_plan,
    norm_gain,
    w_gate,
    w_up,
    w_down,
    expert_ids,
    gate_weights,
    out_grad,
):
    queries, key_rows, value_matrix, out_grad = queries[0], key_rows[0], value_matrix[0], out_grad[0]
    w_gate, w_up, w_down = w_gate[0], w_up[0], w_down[0]
    route_ids, route_gates = expert_ids[0], gate_weights[0]
    x, c, y = lax.axis_index("x"), lax.axis_index("c"), lax.axis_index("y")
    x_size = lax.axis_size("x")
    ranks = 2 * x_size
    rank = x * 2 + c
    count, width = queries.shape
    mask = seq_plan[0, 0]
    gain = norm_gain[None]
    lengths = doc_lengths[0]
    rank_word = jnp.full((1,), rank, jnp.int32)

    units = w_gate.shape[1] // ranks
    pieces = jnp.stack(
        [
            lax.dynamic_slice_in_dim(m, rank * units, units, 0)
            for m in (jnp.transpose(w_gate), jnp.transpose(w_up), w_down)
        ]
    )
    mats = lax.all_gather(pieces, "z", axis=1, tiled=True)

    place = jnp.stack([y, mask]).astype(jnp.int32)
    select, upper, lower, pair_blocks = route(
        *after((place, route_ids, route_gates, out_grad), pieces)
    )
    pair_blocks = to_experts(pair_blocks)
    (select_home,) = by_mask(mask, select)
    pair_block = dense_rows(pair_blocks)
    match = match_of(jnp.stack([x, c]).astype(jnp.int32), pair_blocks, 2 * x_size)
    queries, select_home = after((queries, select_home), (pair_block, match))
    attn, probs, row_blocks = attend(
        lengths, rank_word, queries, key_rows, value_matrix, gain, select_home
    )
    pairs_x = along_x(pair_block)
    row_block = dense_rows(to_experts(row_blocks))
    (grad_home,) = by_mask(mask, after(out_grad, (pairs_x, row_block)))
    row_block, attn_home = after((row_block, attn), grad_home)
    moved = lax.all_gather(attn_home, ("x", "c"))
    hidden_grad = hidden_grad_of(both_cores(pairs_x), mats)
    rows_x, hidden_grad = lax.optimization_barrier((along_x(row_block), hidden_grad))
    rows = both_cores(rows_x)

    far_in, hidden, both = experts_in(rows, mats, match, hidden_grad)
    own_in, own_out, far_out = experts_out(both, hidden, mats)
    in_blocks = add_far(own_in, far_in)
    out_blocks = add_far(*after((own_out, far_out), in_blocks))
    in_parts = half_way(in_blocks)
    out_parts = half_way(out_blocks)
    in_sums = total_of(in_parts)
    in_rows = from_experts(in_sums)
    out_sums = total_of([after(out_parts[0], in_sums[0]), *out_parts[1:]])
    out_rows = from_experts(out_sums)
    in_rows = after(in_rows, out_sums)

    q_home, k_home, v_home = attend_back(
        probs, queries, key_rows, value_matrix, attn, grad_home, gain, select_home, in_rows
    )
    layer = layer_rows(rank_word ^ mask, moved, after(upper, k_home), lower, out_rows)
    return (layer[None], q_home[None], k_home[None], v_home[None])


def solution(mesh):
    fine = Mesh(mesh.devices.reshape(4, 2, 4, 8), ("x", "c", "y", "z"))
    every = ("x", "c", "y", "z")
    expert = ("y", "z")
    return jax.shard_map(
        shards,
        mesh=fine,
        in_specs=(
            P(every),
            P(every),
            P(every),
            P(expert),
            P(expert),
            P(),
            P(expert),
            P(expert),
            P(expert),
            P(every),
            P(every),
            P(every),
        ),
        out_specs=(P(every), P(every), P(every), P(every)),
        check_vma=False,
    )
```

```python
import functools

import jax
import jax.numpy as jnp
from jax import lax
from jax.experimental import pallas as pl
from jax.experimental.pallas import tpu as pltpu
from jax.sharding import Mesh
from jax.sharding import PartitionSpec as P

HEAD_SIZE = 128
QUERY_HEADS = 32
KEY_VALUE_HEADS = 2
CAP = 14
ROWS = 16
EXPERTS = 4
HEADS_AT_ONCE = 16
SPAN = HEADS_AT_ONCE * HEAD_SIZE
SCALE = HEAD_SIZE ** (-0.5)
F32 = jnp.float32
BF16 = jnp.bfloat16
MIB = 1 << 20


def nt(left, right):
    return lax.dot_general(left, right, (((1,), (1,)), ((), ())), preferred_element_type=F32)


def tn(left, right):
    return lax.dot_general(left, right, (((0,), (0,)), ((), ())), preferred_element_type=F32)


def nn(left, right):
    return jnp.dot(left, right, preferred_element_type=F32)


def stacked(wide):
    return jnp.concatenate(
        [wide[:, i * HEAD_SIZE : (i + 1) * HEAD_SIZE] for i in range(HEADS_AT_ONCE)], axis=0
    )


def side_by_side(tall):
    count = tall.shape[0] // HEADS_AT_ONCE
    return jnp.concatenate(
        [tall[i * count : (i + 1) * count] for i in range(HEADS_AT_ONCE)], axis=1
    )


def allowed_keys(lengths_ref, rank_ref, count):
    rank = rank_ref[0]
    here = lax.broadcasted_iota(jnp.int32, (count, count), 0)
    there = lax.broadcasted_iota(jnp.int32, (count, count), 1)
    bound = jnp.int32(0)
    mine = jnp.zeros((count, count), jnp.int32)
    other = jnp.zeros((count, count), jnp.int32)
    for i in range(lengths_ref.shape[1]):
        bound = bound + lengths_ref[rank, i]
        mine = mine + (here >= bound).astype(jnp.int32)
        other = other + (there >= bound).astype(jnp.int32)
    allowed = (mine == other) & (there <= here)
    return jnp.concatenate([allowed.astype(jnp.int32)] * HEADS_AT_ONCE, axis=0) > 0


def softmax_rows(tall, k_part, allowed):
    scores = jnp.where(allowed, nt(tall, k_part) * SCALE, -1e30)
    expo = jnp.exp(scores - jnp.max(scores, axis=-1, keepdims=True))
    return expo / jnp.sum(expo, axis=-1, keepdims=True)


def head_part(ref, step):
    steps = QUERY_HEADS // (KEY_VALUE_HEADS * HEADS_AT_ONCE)
    return ref[:, pl.ds(pl.multiple_of(step // steps * HEAD_SIZE, HEAD_SIZE), HEAD_SIZE)]


def span_of(step):
    return pl.ds(pl.multiple_of(step * SPAN, SPAN), SPAN)


def route_kernel(
    place_ref, ids_ref, gates_ref, grad_ref, select_ref, upper_ref, lower_ref, *pair_refs
):
    count = ids_ref.shape[0]
    ids, gates = ids_ref[...], gates_ref[...]
    here = lax.broadcasted_iota(jnp.int32, (count, count), 0)
    there = lax.broadcasted_iota(jnp.int32, (count, count), 1)
    group, slot = there // ROWS, there % ROWS
    present = jnp.zeros((count, count), F32)
    weight = jnp.zeros((count, count), F32)
    for i in range(EXPERTS):
        hit = ids == lax.rem(place_ref[0] + i, EXPERTS)
        found = jnp.max(hit.astype(F32), axis=-1, keepdims=True)
        amount = jnp.sum(jnp.where(hit, gates, 0.0), axis=-1, keepdims=True)
        present = jnp.where(group == i, found, present)
        weight = jnp.where(group == i, amount, weight)
    counts = nn((there < here).astype(BF16), present.astype(BF16))
    select = (present > 0.5) & (counts == slot.astype(F32))
    chosen = select.astype(F32).astype(BF16)
    select_ref[...] = chosen
    spread = jnp.where(select, weight, 0.0)
    upper = spread.astype(BF16)
    upper_ref[...] = upper
    lower_ref[...] = (spread - upper.astype(F32)).astype(BF16)
    total = EXPERTS * ROWS
    slot_weight = jnp.sum(jnp.transpose(spread), axis=-1, keepdims=True)[:total]
    picker = jnp.transpose(select.astype(F32))[:total].astype(BF16)
    line = lax.broadcasted_iota(jnp.int32, (total, 1), 0) % ROWS
    mark = jnp.where(line == ROWS - 1, place_ref[1].astype(F32), 0.0)

    def gather(step, carry):
        rows = (slot_weight * nn(picker, grad_ref[:, span_of(step)]) + mark).astype(BF16)
        for i, pair_ref in enumerate(pair_refs):
            pair_ref[:, span_of(step)] = rows[i * ROWS : (i + 1) * ROWS]
        return carry

    lax.fori_loop(0, grad_ref.shape[1] // SPAN, gather, 0)


def forward_kernel(
    lengths_ref, rank_ref, q_ref, k_ref, v_ref, gain_ref, select_ref, attn_ref, probs_ref, *row_refs
):
    count, width = q_ref.shape
    allowed = allowed_keys(lengths_ref, rank_ref, count)

    def heads(step, total):
        probs = softmax_rows(stacked(q_ref[:, span_of(step)]), head_part(k_ref, step), allowed)
        probs = probs.astype(BF16)
        probs_ref[step] = probs
        mixed = side_by_side(nn(probs, head_part(v_ref, step))).astype(BF16)
        attn_ref[:, span_of(step)] = mixed
        wide = mixed.astype(F32)
        return total + jnp.sum(wide * wide, axis=-1, keepdims=True)

    total = lax.fori_loop(0, width // SPAN, heads, jnp.zeros((count, 1), F32))
    scaling = lax.rsqrt(total / width + 1e-06)
    slots = EXPERTS * ROWS
    picker = jnp.transpose(select_ref[...].astype(F32))[:slots].astype(BF16)

    def norm(step, carry):
        wide = attn_ref[:, span_of(step)].astype(F32)
        normed = (wide * scaling * gain_ref[:, span_of(step)]).astype(BF16)
        rows = nn(picker, normed).astype(BF16)
        for i, row_ref in enumerate(row_refs):
            row_ref[:, span_of(step)] = rows[i * ROWS : (i + 1) * ROWS]
        return carry

    lax.fori_loop(0, width // SPAN, norm, 0)


def backward_kernel(
    probs_ref,
    q_ref,
    k_ref,
    v_ref,
    attn_ref,
    grad_ref,
    gain_ref,
    spread_ref,
    in0_ref,
    in1_ref,
    in2_ref,
    in3_ref,
    q_out,
    k_out,
    v_out,
    normed_grad,
):
    count, width = q_ref.shape
    in_refs = (in0_ref, in1_ref, in2_ref, in3_ref)

    def gather(step, carry):
        square, product = carry
        span = span_of(step)
        rows = jnp.concatenate([ref[:, span] for ref in in_refs], axis=0)
        grad = nn(spread_ref[:, : EXPERTS * ROWS], rows)
        normed_grad[:, span] = grad
        wide = attn_ref[:, span].astype(F32)
        square = square + jnp.sum(wide * wide, axis=-1, keepdims=True)
        product = product + jnp.sum(wide * gain_ref[:, span] * grad, axis=-1, keepdims=True)
        return square, product

    zero = jnp.zeros((count, 1), F32)
    square, product = lax.fori_loop(0, width // SPAN, gather, (zero, zero))
    scaling = lax.rsqrt(square / width + 1e-06)
    lost = scaling * scaling * scaling * (product / width)
    k_sums = [jnp.zeros((count, HEAD_SIZE), F32)] * KEY_VALUE_HEADS
    v_sums = [jnp.zeros((count, HEAD_SIZE), F32)] * KEY_VALUE_HEADS
    steps = width // SPAN // KEY_VALUE_HEADS

    for head in range(KEY_VALUE_HEADS):
        part = slice(head * HEAD_SIZE, (head + 1) * HEAD_SIZE)

        def heads(turn, sums, head=head, part=part):
            step = turn + head * steps
            span = span_of(step)
            k_part, v_part = k_ref[:, part], v_ref[:, part]
            wide = attn_ref[:, span].astype(F32)
            attn_grad = (
                grad_ref[:, span].astype(F32)
                + scaling * gain_ref[:, span] * normed_grad[:, span]
                - wide * lost
            ).astype(BF16)
            tall_q, tall_d = stacked(q_ref[:, span]), stacked(attn_grad)
            probs = probs_ref[step]
            inner = stacked(attn_grad.astype(F32) * wide)
            inner = jnp.sum(inner, axis=-1, keepdims=True)
            score_grad = probs.astype(F32) * (nt(tall_d, v_part) - inner) * SCALE
            score_grad = score_grad.astype(BF16)
            q_out[:, span] = side_by_side(nn(score_grad, k_part)).astype(BF16)
            return sums[0] + tn(score_grad, tall_q), sums[1] + tn(probs, tall_d)

        zeros = jnp.zeros((count, HEAD_SIZE), F32)
        k_sum, v_sum = lax.fori_loop(0, steps, heads, (zeros, zeros))
        k_out[:, part] = k_sum.astype(BF16)
        v_out[:, part] = v_sum.astype(BF16)


def cost(micros):
    return pl.CostEstimate(
        flops=int(micros * 1.15e9), bytes_accessed=int(micros * 3.6e6), transcendentals=0
    )


def whole():
    return pl.BlockSpec(memory_space=pltpu.VMEM)


def scalars():
    return pl.BlockSpec(memory_space=pltpu.SMEM)


def shape(*dims, dtype=BF16):
    return jax.ShapeDtypeStruct(dims, dtype)


def route(place, ids, gates, grad):
    count, width = grad.shape
    out = pl.pallas_call(
        route_kernel,
        out_shape=[shape(count, count)] * 3 + [shape(ROWS, width)] * EXPERTS,
        in_specs=[scalars()] + [whole()] * 3,
        out_specs=[whole()] * (3 + EXPERTS),
        compiler_params=pltpu.CompilerParams(vmem_limit_bytes=16 * MIB),
        cost_estimate=cost(2.5),
        name="route",
    )(place, ids, gates, grad)
    return *out[:3], list(out[3:])


def attend(lengths, rank, queries, key_rows, value_matrix, gain, select):
    count, width = queries.shape
    out = pl.pallas_call(
        forward_kernel,
        out_shape=[
            shape(count, width),
            shape(QUERY_HEADS // HEADS_AT_ONCE, HEADS_AT_ONCE * count, count),
            *([shape(ROWS, width)] * EXPERTS),
        ],
        in_specs=[scalars()] * 2 + [whole()] * 5,
        out_specs=[whole()] * (2 + EXPERTS),
        compiler_params=pltpu.CompilerParams(vmem_limit_bytes=24 * MIB),
        cost_estimate=cost(4.6),
        name="attend",
    )(lengths, rank, queries, key_rows, value_matrix, gain, select)
    return out[0], out[1], list(out[2:])


def attend_back(probs, queries, key_rows, value_matrix, attn, grad, gain, spread, in_rows):
    count, width = queries.shape
    return pl.pallas_call(
        backward_kernel,
        out_shape=[shape(count, width), shape(*key_rows.shape), shape(*key_rows.shape)],
        in_specs=[whole()] * (8 + EXPERTS),
        out_specs=[whole()] * 3,
        scratch_shapes=[pltpu.VMEM((count, width), F32)],
        compiler_params=pltpu.CompilerParams(vmem_limit_bytes=32 * MIB),
        cost_estimate=cost(5),
        name="attend_back",
    )(probs, queries, key_rows, value_matrix, attn, grad, gain, spread, *in_rows)


CHUNK = 2048


def dense_kernel(*refs):
    *in_refs, out_ref = refs
    out_ref[...] = jnp.concatenate([ref[:CAP].astype(F32) for ref in in_refs], axis=0).astype(BF16)


def by_columns(kernel, name, inputs, outs, chunk=CHUNK):
    width = inputs[0].shape[1]
    return pl.pallas_call(
        kernel,
        grid=(width // chunk,),
        in_specs=[pl.BlockSpec((v.shape[0], chunk), lambda i: (0, i)) for v in inputs],
        out_specs=[pl.BlockSpec((rows, chunk), lambda i: (0, i)) for rows in outs],
        out_shape=[shape(rows, width) for rows in outs],
        compiler_params=pltpu.CompilerParams(vmem_limit_bytes=16 * MIB),
        cost_estimate=pl.CostEstimate(
            flops=0,
            bytes_accessed=2 * width * (sum(outs) + sum(v.shape[0] for v in inputs)),
            transcendentals=0,
        ),
        name=name,
    )(*inputs)


def dense_rows(blocks):
    return by_columns(dense_kernel, "dense_rows", blocks, [CAP * EXPERTS])[0]


def add_kernel(own_ref, far_ref, *out_refs):
    total = own_ref[...].astype(F32) + far_ref[...].astype(F32)
    start = 0
    for out_ref in out_refs:
        out_ref[...] = total[start : start + out_ref.shape[0]].astype(BF16)
        start += out_ref.shape[0]


def relay_kernel(left_ref, right_ref, top_ref, low_ref, left_out, right_out):
    left, right = left_ref[...].astype(F32), right_ref[...].astype(F32)
    top = top_ref.shape[0]
    left_out[...] = jnp.concatenate(
        [left[:top] + top_ref[...].astype(F32), left[top:]], axis=0
    ).astype(BF16)
    right_out[...] = jnp.concatenate(
        [right[:top], right[top:] + low_ref[...].astype(F32)], axis=0
    ).astype(BF16)


def sum_kernel(*refs):
    in_refs, out_refs = refs[:-EXPERTS], refs[-EXPERTS:]
    total = in_refs[0][...].astype(F32)
    for ref in in_refs[1:]:
        total = total + ref[...].astype(F32)
    for i, out_ref in enumerate(out_refs):
        block = total[i * CAP : (i + 1) * CAP]
        empty = jnp.zeros((ROWS - CAP, block.shape[1]), F32)
        out_ref[...] = jnp.concatenate([block, empty], axis=0).astype(BF16)


def match_kernel(place_ref, *refs):
    *mark_refs, out_ref = refs
    total = out_ref.shape[0]
    size = total // (2 * CAP * EXPERTS)

    def keys(dims, axis, marked):
        index = lax.broadcasted_iota(jnp.int32, dims, axis)
        block, turn = index // (CAP * EXPERTS), index // CAP % EXPERTS
        away, flip = block % size, block // size
        owner = (place_ref[0] + size - away) % size * 2 + (place_ref[1] ^ flip)
        if marked:
            mask = jnp.zeros(dims, jnp.int32)
            for i, ref in enumerate(mark_refs):
                mark = ref[ROWS - 1 :, :1].astype(F32).astype(jnp.int32)
                mask = jnp.where(turn == i, mark, mask)
            owner = owner ^ mask
        return owner * (CAP * EXPERTS) + index % (CAP * EXPERTS)

    same = keys((total, 1), 0, True) == keys((1, total), 1, False)
    out_ref[...] = same.astype(F32).astype(BF16)


def match_of(place, blocks, devices):
    total = devices * CAP * EXPERTS
    return pl.pallas_call(
        match_kernel,
        grid=(1,),
        in_specs=[
            pl.BlockSpec(memory_space=pltpu.SMEM),
            *([pl.BlockSpec((ROWS, HEAD_SIZE), lambda i: (0, 0))] * len(blocks)),
        ],
        out_specs=pl.BlockSpec((total, total), lambda i: (0, 0)),
        out_shape=shape(total, total),
        compiler_params=pltpu.CompilerParams(vmem_limit_bytes=16 * MIB),
        cost_estimate=cost(1),
        name="match",
    )(place, *blocks)


def layer_kernel(home_ref, moved_ref, upper_ref, lower_ref, *refs):
    *in_refs, out_ref = refs
    rows = jnp.concatenate([ref[...] for ref in in_refs], axis=0)
    slots = rows.shape[0]
    added = nn(upper_ref[:, :slots], rows) + nn(lower_ref[:, :slots], rows)
    out_ref[...] = (moved_ref[0].astype(F32) + added).astype(BF16)


def layer_rows(home, moved, upper, lower, rows):
    _, count, width = moved.shape
    wide = lambda n: pl.BlockSpec((n, CHUNK), lambda i, home: (0, i))
    fixed = pl.BlockSpec(upper.shape, lambda i, home: (0, 0))
    return pl.pallas_call(
        layer_kernel,
        grid_spec=pltpu.PrefetchScalarGridSpec(
            num_scalar_prefetch=1,
            grid=(width // CHUNK,),
            in_specs=[
                pl.BlockSpec((1, count, CHUNK), lambda i, home: (home[0], 0, i)),
                fixed,
                fixed,
                *([wide(ROWS)] * EXPERTS),
            ],
            out_specs=wide(count),
        ),
        out_shape=shape(count, width),
        compiler_params=pltpu.CompilerParams(vmem_limit_bytes=58 * MIB),
        cost_estimate=cost(4),
        name="layer_rows",
    )(home, moved, upper, lower, *rows)


def joined(refs):
    return jnp.concatenate([ref[...].astype(F32) for ref in refs], axis=0).astype(BF16)


def hidden_grad_kernel(*refs):
    *grad_refs, mats_ref, out_ref = refs

    @pl.when(pl.program_id(0) == 0)
    def _():
        out_ref[...] = jnp.zeros_like(out_ref)

    out_ref[...] += nt(joined(grad_refs), mats_ref[0])


def hidden_grad_of(grads, mats):
    each, width = grads[0].shape
    total, units = len(grads) * each, mats.shape[1]
    return pl.pallas_call(
        hidden_grad_kernel,
        grid=(width // CHUNK,),
        in_specs=[
            *([pl.BlockSpec((each, CHUNK), lambda i: (0, i))] * len(grads)),
            pl.BlockSpec((1, units, CHUNK), lambda i: (2, 0, i)),
        ],
        out_specs=pl.BlockSpec((total, units), lambda i: (0, 0)),
        out_shape=shape(total, units, dtype=F32),
        compiler_params=pltpu.CompilerParams(vmem_limit_bytes=58 * MIB),
        cost_estimate=cost(4),
        name="hidden_grad",
    )(*grads, mats)


def experts_in_kernel(steps, blocks, *refs):
    row_refs = refs[:blocks]
    mats_ref, match_ref, hidden_grad, far_ref, hidden_ref, own_ref = refs[blocks : blocks + 6]
    gate_in, up_in, both = refs[blocks + 6 :]
    step = pl.program_id(0)
    units = mats_ref.shape[1]

    @pl.when(step == 0)
    def _():
        gate_in[...] = jnp.zeros_like(gate_in)
        up_in[...] = jnp.zeros_like(up_in)

    @pl.when(step < steps)
    def _():
        rows = joined(row_refs)
        gate_in[...] += nt(rows, mats_ref[0])
        up_in[...] += nt(rows, mats_ref[1])

    @pl.when(step == steps - 1)
    def _():
        match = match_ref[...]
        rest = hidden_grad[...]
        grad = jnp.zeros_like(rest)
        for _ in range(3):
            piece = rest.astype(BF16)
            grad = grad + nn(match, piece)
            rest = rest - piece.astype(F32)
        gate = gate_in[...]
        up = up_in[...]
        sigma = jax.nn.sigmoid(gate)
        active = gate * sigma
        hidden_ref[...] = tn(match, (active * up).astype(BF16)).astype(BF16)
        both[:, :units] = (grad * up * sigma * (1.0 + gate * (1.0 - sigma))).astype(BF16)
        both[:, units:] = (grad * active).astype(BF16)
        own_ref[...] = both[: own_ref.shape[0]]

    @pl.when(step >= steps)
    def _():
        mats = jnp.concatenate([mats_ref[0], mats_ref[1]], axis=0)
        far_ref[...] = nn(both[far_ref.shape[0] :], mats).astype(BF16)


def experts_in(rows, mats, match, hidden_grad):
    blocks = len(rows)
    each, width = rows[0].shape
    total = blocks * each
    units = mats.shape[1]
    steps = width // CHUNK
    half = total // 2
    first = lambda i: (0, jnp.minimum(i, steps - 1))
    last = lambda i: (0, jnp.maximum(i - steps, 0))
    fixed = lambda i: (0, 0)
    return pl.pallas_call(
        functools.partial(experts_in_kernel, steps, blocks),
        grid=(2 * steps,),
        in_specs=[
            *([pl.BlockSpec((each, CHUNK), first)] * blocks),
            pl.BlockSpec((2, units, CHUNK), lambda i: (0, 0, lax.rem(i, steps))),
            pl.BlockSpec((total, total), fixed),
            pl.BlockSpec((total, units), fixed),
        ],
        out_specs=[
            pl.BlockSpec((half, CHUNK), last),
            pl.BlockSpec((total, units), fixed),
            pl.BlockSpec((half, 2 * units), fixed),
        ],
        out_shape=[shape(half, width), shape(total, units), shape(half, 2 * units)],
        scratch_shapes=[pltpu.VMEM((total, units), F32)] * 2 + [pltpu.VMEM((total, 2 * units), BF16)],
        compiler_params=pltpu.CompilerParams(vmem_limit_bytes=58 * MIB),
        cost_estimate=cost(10),
        name="experts_in",
    )(*rows, mats, match, hidden_grad)


def experts_out_kernel(both_ref, hidden_ref, mats_ref, own_in, own_out, far_out):
    half = own_out.shape[0]
    gates = jnp.concatenate([mats_ref[0], mats_ref[1]], axis=0)
    own_in[...] = nn(both_ref[...], gates).astype(BF16)
    far_out[...] = nn(hidden_ref[half:], mats_ref[2]).astype(BF16)
    own_out[...] = nn(hidden_ref[:half], mats_ref[2]).astype(BF16)


def experts_out(both, hidden, mats):
    half, units = both.shape[0], mats.shape[1]
    width = mats.shape[2]
    return pl.pallas_call(
        experts_out_kernel,
        grid=(width // CHUNK,),
        in_specs=[
            pl.BlockSpec(both.shape, lambda i: (0, 0)),
            pl.BlockSpec(hidden.shape, lambda i: (0, 0)),
            pl.BlockSpec((3, units, CHUNK), lambda i: (0, 0, i)),
        ],
        out_specs=[pl.BlockSpec((half, CHUNK), lambda i: (0, i))] * 3,
        out_shape=[shape(half, width)] * 3,
        compiler_params=pltpu.CompilerParams(vmem_limit_bytes=58 * MIB),
        cost_estimate=cost(5),
        name="experts_out",
    )(both, hidden, mats)


def shifted(value, axis, step):
    size = lax.axis_size(axis)
    if step % size == 0:
        return value
    return lax.ppermute(value, axis, [(i, (i + step) % size) for i in range(size)])


def swapped(value):
    return lax.ppermute(value, "c", [(0, 1), (1, 0)])


def to_experts(blocks):
    return [shifted(blocks[s], "y", s) for s in range(EXPERTS)]


def from_experts(blocks):
    return [shifted(blocks[s], "y", -s) for s in range(EXPERTS)]


def along_x(block):
    moved = {s: shifted(block, "x", s) for s in (2, 1, 3)}
    return [block, moved[1], moved[2], moved[3]]


def both_cores(blocks):
    return blocks + [swapped(b) for b in blocks]


TOP = 32


def add_far(own, far):
    each = own.shape[0] // lax.axis_size("x")
    sizes = [each, each, TOP, each - TOP, each]
    return by_columns(add_kernel, "add_rows", [own, swapped(far)], sizes)


def half_way(blocks):
    mine, left, top, low, right = blocks
    parts = [left, right, shifted(top, "x", -1), shifted(low, "x", 1)]
    left, right = by_columns(relay_kernel, "relay_rows", parts, [left.shape[0]] * 2)
    return [mine, shifted(left, "x", -1), shifted(right, "x", 1)]


def total_of(parts):
    return by_columns(sum_kernel, "sum_rows", parts, [ROWS] * EXPERTS)


def by_mask(mask, *values):
    ranks = lax.axis_size("x") * lax.axis_size("c")

    def branch(k):
        pairs = [(i, i ^ k) for i in range(ranks)]
        return lambda *v: tuple(lax.ppermute(one, ("x", "c"), pairs) for one in v)

    return lax.switch(mask - 1, [branch(k) for k in range(1, ranks)], *values)


def after(values, other):
    return lax.optimization_barrier((values, other))[0]


def shards(
    queries,
    key_rows,
    value_matrix,
    doc_lengths,
    seq_plan,
    norm_gain,
    w_gate,
    w_up,
    w_down,
    expert_ids,
    gate_weights,
    out_grad,
):
    queries, key_rows, value_matrix, out_grad = queries[0], key_rows[0], value_matrix[0], out_grad[0]
    w_gate, w_up, w_down = w_gate[0], w_up[0], w_down[0]
    route_ids, route_gates = expert_ids[0], gate_weights[0]
    x, c, y = lax.axis_index("x"), lax.axis_index("c"), lax.axis_index("y")
    x_size = lax.axis_size("x")
    ranks = 2 * x_size
    rank = x * 2 + c
    count, width = queries.shape
    mask = seq_plan[0, 0]
    gain = norm_gain[None]
    lengths = doc_lengths[0]
    rank_word = jnp.full((1,), rank, jnp.int32)

    units = w_gate.shape[1] // ranks
    pieces = jnp.stack(
        [
            lax.dynamic_slice_in_dim(m, rank * units, units, 0)
            for m in (jnp.transpose(w_gate), jnp.transpose(w_up), w_down)
        ]
    )
    mats = lax.all_gather(pieces, "z", axis=1, tiled=True)

    place = jnp.stack([y, mask]).astype(jnp.int32)
    select, upper, lower, pair_blocks = route(
        *after((place, route_ids, route_gates, out_grad), pieces)
    )
    pair_blocks = to_experts(pair_blocks)
    (select_home,) = by_mask(mask, select)
    pair_block = dense_rows(pair_blocks)
    match = match_of(jnp.stack([x, c]).astype(jnp.int32), pair_blocks, 2 * x_size)
    queries, select_home = after((queries, select_home), (pair_block, match))
    attn, probs, row_blocks = attend(
        lengths, rank_word, queries, key_rows, value_matrix, gain, select_home
    )
    pairs_x = along_x(pair_block)
    row_block = dense_rows(to_experts(row_blocks))
    (grad_home,) = by_mask(mask, after(out_grad, (pairs_x, row_block)))
    row_block, attn_home = after((row_block, attn), grad_home)
    moved = lax.all_gather(attn_home, ("x", "c"))
    hidden_grad = hidden_grad_of(both_cores(pairs_x), mats)
    rows_x, hidden_grad = lax.optimization_barrier((along_x(row_block), hidden_grad))
    rows = both_cores(rows_x)

    far_in, hidden, both = experts_in(rows, mats, match, hidden_grad)
    own_in, own_out, far_out = experts_out(both, hidden, mats)
    in_blocks = add_far(own_in, far_in)
    out_blocks = add_far(*after((own_out, far_out), in_blocks))
    in_parts = half_way(in_blocks)
    out_parts = half_way(out_blocks)
    in_sums = total_of(in_parts)
    in_rows = from_experts(in_sums)
    out_sums = total_of([after(out_parts[0], in_sums[0]), *out_parts[1:]])
    out_rows = from_experts(out_sums)
    in_rows = after(in_rows, out_sums)

    q_home, k_home, v_home = attend_back(
        probs, queries, key_rows, value_matrix, attn, grad_home, gain, select_home, in_rows
    )
    layer = layer_rows(rank_word ^ mask, moved, after(upper, k_home), lower, out_rows)
    return (layer[None], q_home[None], k_home[None], v_home[None])


def solution(mesh):
    fine = Mesh(mesh.devices.reshape(4, 2, 4, 8), ("x", "c", "y", "z"))
    every = ("x", "c", "y", "z")
    expert = ("y", "z")
    return jax.shard_map(
        shards,
        mesh=fine,
        in_specs=(
            P(every),
            P(every),
            P(every),
            P(expert),
            P(expert),
            P(),
            P(expert),
            P(expert),
            P(expert),
            P(every),
            P(every),
            P(every),
        ),
        out_specs=(P(every), P(every), P(every), P(every)),
        check_vma=False,
    )
```
